256 devices in a mesh: seq: 2 (over core), row: 16 (over y, x), head: 8 (over z).
Axes of the slice: x: 4, y: 4, z: 8, core: 2. Of those that a mesh axis runs over, the one named last changes fastest.
Arguments:
- seq_in: bfloat16 [24576, 10240], P(('seq', 'row'), 'head'), may hold values from -6 to 6
- gate_in: bfloat16 [24576, 10240], P(('seq', 'row'), 'head'), may hold values from -6 to 6
- b_in: bfloat16 [24576, 128], P(('seq', 'row')), may hold values from -0.5 to 0.5
- c_in: bfloat16 [24576, 128], P(('seq', 'row')), may hold values from -6 to 6
- step: float32 [80, 24576], P('head', ('seq', 'row')), may hold values from 0 to 1, as said below
- log_gate: float32 [80, 24576], P('head', ('seq', 'row')), may hold values from -1 to 0, as said below
- skip: float32 [80], P('head'), may hold values from 0.2 to 0.6
- out_weight: bfloat16 [2560, 10240], P(('seq', 'row'), 'head'), may hold values from -0.0625 to 0.0625
Outputs:
- result_out: bfloat16 [24576, 2560], P(('seq', 'row'), 'head')
The draws below stay inside these ranges and needn't reach their ends.
Inputs may be any that keep to these rules, and one draw needn't show every extreme that they name: `step`: positive. `log_gate`: at most zero.
All inputs are finite; a program needn't handle non-finite values.
Results may differ from the reference program's by a relative error of at most 0.022.
Values may be sent and summed in bfloat16 or wider, within the bound.
No kernel may reach another device: no remote copies, remote signals or barrier semaphores. Data moves between devices by JAX's collectives and lax.ppermute only.
A program may use at most 128 MiB of HBM per device.

```python
import math
import jax
import jax.numpy as jnp
from jax import lax

SPACE_HEADS = 80
P_SIZE = 128
N = 128
DW = 2560
BLK = 128
TOK_DEV = 768
SEQUENCE_TOKENS = 24576
HP = 10240
N_HEAD = 8


def draw_step(key, part):
    key = jax.random.fold_in(key, 5)
    scale_base = 2.0 / math.sqrt(SEQUENCE_TOKENS)
    factor = jnp.exp(jax.random.uniform(key, (SPACE_HEADS, SEQUENCE_TOKENS), minval=math.log(0.5), maxval=math.log(2.0)))
    return (scale_base * factor).astype(jnp.float32)


def draw_log_gate(key, part):
    key = jax.random.fold_in(key, 7)
    random_split_keys = jax.random.split(key, 7)
    fraction = 0.5
    quick_heads = jax.random.uniform(random_split_keys[0], (SPACE_HEADS,)) < fraction
    quick_rates = 1.0 / jax.random.uniform(random_split_keys[1], (SPACE_HEADS,), minval=30.0, maxval=50.0)
    slow_rates = jax.random.uniform(random_split_keys[2], (SPACE_HEADS,), minval=0.15, maxval=0.5) / SEQUENCE_TOKENS
    rates = jnp.where(quick_heads, quick_rates, slow_rates)
    shard_factor = jnp.exp(jax.random.uniform(random_split_keys[3], (SEQUENCE_TOKENS // TOK_DEV,), minval=math.log(0.5), maxval=math.log(2.0)))
    shard_factor = jnp.repeat(shard_factor, TOK_DEV)
    roughness = jax.random.uniform(random_split_keys[4], (SPACE_HEADS, SEQUENCE_TOKENS), minval=0.5, maxval=1.5)
    logarithm_decay_rates = -rates[:, None] * shard_factor[None, :] * roughness
    spike_positions = jax.random.randint(random_split_keys[5], (3,), 0, SEQUENCE_TOKENS)
    spike_decay_loss = jax.random.uniform(random_split_keys[6], (3, SPACE_HEADS), minval=0.2, maxval=0.4)
    spike_token_hits = (jnp.arange(SEQUENCE_TOKENS)[None, :] == spike_positions[:, None]).astype(jnp.float32)
    logarithm_decay_rates = logarithm_decay_rates + jnp.sum(jnp.log(1.0 - spike_decay_loss)[:, :, None] * spike_token_hits[:, None, :], axis=0)
    return logarithm_decay_rates.astype(jnp.float32)


def block_scale(rng, shape, cuts, low, high):
    def one(axis_at, blocks):
        heights = jax.random.uniform(jax.random.fold_in(jax.random.fold_in(rng, 6), axis_at), (blocks,), jnp.float32, low / len(cuts), high / len(cuts))
        return jnp.repeat(jnp.exp(heights), shape[axis_at] // blocks).reshape((-1,) + (1,) * (len(shape) - axis_at - 1))

    loudness = one(*cuts[0])
    for cut in cuts[1:]:
        loudness = loudness * one(*cut)
    return loudness


def noise(rng, shape, scale, most, cuts=(), held_as=jnp.bfloat16):
    gain = block_scale(rng, shape, cuts, -0.22, 0.18) if cuts else 1.0
    array = jax.random.normal(rng, shape, jnp.float32) * scale * gain
    return jnp.minimum(jnp.maximum(array, -most), most).astype(held_as)


def setup_inputs(seed: int = 0) -> dict:
    key_of = jax.random.split(jax.random.key(seed), 9)
    seq_in = noise(key_of[0], (SEQUENCE_TOKENS, HP), 1.0, 6.0, ((0, 32), (1, 8)))
    gate_in = noise(key_of[1], (SEQUENCE_TOKENS, HP), 1.0, 6.0, ((0, 32), (1, 8)))
    b_in = noise(key_of[2], (SEQUENCE_TOKENS, N), N ** -0.5, 0.5, ((0, 32),))
    c_in = noise(key_of[3], (SEQUENCE_TOKENS, N), 1.0, 6.0, ((0, 32),))
    step = draw_step(jax.random.fold_in(key_of[8], 71), 0)
    log_gate = draw_log_gate(jax.random.fold_in(key_of[8], 71), 0)
    skip = jnp.clip(0.2 + 0.400000021 * jax.random.uniform(key_of[6], (SPACE_HEADS,), jnp.float32) ** block_scale(key_of[6], (SPACE_HEADS,), ((0, 8),), -0.2, 0.2), 0.2, 0.6)
    out_weight = noise(key_of[7], (DW, HP), HP ** -0.5, 0.0625, ((0, 32), (1, 8)))
    return {"seq_in": seq_in, "gate_in": gate_in, "b_in": b_in, "c_in": c_in, "step": step, "log_gate": log_gate, "skip": skip, "out_weight": out_weight}


def reference(seq_in, gate_in, b_in, c_in, step, log_gate, skip, out_weight):
    block_count = SEQUENCE_TOKENS // BLK
    input_blocks = seq_in.reshape(block_count, BLK, SPACE_HEADS, P_SIZE)
    gate_blocks = gate_in.reshape(block_count, BLK, SPACE_HEADS * P_SIZE)
    b_blocks = b_in.reshape(block_count, BLK, N)
    c_blocks = c_in.reshape(block_count, BLK, N)
    step_blocks = step.reshape(SPACE_HEADS, block_count, BLK).transpose(1, 0, 2)
    gate_logs = log_gate.reshape(SPACE_HEADS, block_count, BLK).transpose(1, 0, 2)
    weight_groups = out_weight.reshape(DW, N_HEAD, SPACE_HEADS * P_SIZE // N_HEAD).astype(jnp.float32)
    position = jnp.arange(BLK)
    causal = position[:, None] >= position[None, :]

    def advance_block(carried, element):
        inputs, gates, b_rows, c_rows, steps_blk, logs_blk = element
        running = jnp.cumsum(logs_blk, axis=1)
        log_span = running[:, :, None] - running[:, None, :]
        decays = jnp.where(causal[None], jnp.exp(jnp.where(causal[None], log_span, 0.0)), 0.0)
        scores = jnp.dot(c_rows, b_rows.T, preferred_element_type=jnp.float32)
        weight = (decays * scores[None] * steps_blk[:, None, :]).astype(jnp.bfloat16)
        inner_out = jnp.einsum('hij,jhp->ihp', weight.astype(jnp.float32), inputs.astype(jnp.float32))
        carried_out = jnp.exp(running).T[:, :, None] * jnp.einsum(
            'in,hpn->ihp', c_rows.astype(jnp.float32), carried, precision=lax.Precision.HIGHEST)
        mixture = inner_out + carried_out + skip[None, :, None] * inputs.astype(jnp.float32)
        hidden = (mixture.reshape(BLK, SPACE_HEADS * P_SIZE) * jax.nn.silu(gates.astype(jnp.float32))).astype(jnp.bfloat16)
        tail_decay = jnp.exp(running[:, -1:] - running) * steps_blk
        scaled = (tail_decay.T[:, :, None] * inputs.astype(jnp.float32)).astype(jnp.bfloat16)
        block_state = jnp.einsum('jhp,jn->hpn', scaled.astype(jnp.float32), b_rows.astype(jnp.float32))
        carried = jnp.exp(running[:, -1])[:, None, None] * carried + block_state
        parts = jnp.einsum('tgk,dgk->gtd', hidden.reshape(BLK, N_HEAD, SPACE_HEADS * P_SIZE // N_HEAD).astype(jnp.float32),
                           weight_groups).astype(jnp.bfloat16)
        block_out = jnp.sum(parts.astype(jnp.float32), axis=0).astype(jnp.bfloat16)
        return carried, block_out

    initial = jnp.zeros((SPACE_HEADS, P_SIZE, N), jnp.float32)
    final_state, outputs = lax.scan(advance_block, initial,
                                    (input_blocks, gate_blocks, b_blocks, c_blocks, step_blocks, gate_logs))
    return outputs.reshape(SEQUENCE_TOKENS, DW)
```

```python
import jax
import jax.numpy as jnp
from jax import lax
from jax.experimental import pallas as pl
from jax.experimental.pallas import tpu as pltpu
from jax.sharding import PartitionSpec as P

P_SIZE = 128
N = 128
BLK = 128
TOK = 768
HEADS = 10
CH = HEADS * P_SIZE
HALF = CH // 2
SHARDS = 32
NBLK = TOK // BLK
F32 = jnp.float32
BF16 = jnp.bfloat16
HIGH = lax.Precision.HIGHEST
NT = (((1,), (1,)), ((), ()))
TN = (((0,), (0,)), ((), ()))


def triangle(upto):
    rows = lax.broadcasted_iota(jnp.int32, (BLK, BLK), 0)
    cols = lax.broadcasted_iota(jnp.int32, (BLK, BLK), 1)
    return jnp.where(upto(rows, cols), 1.0, 0.0).astype(F32)


def split3(value):
    high = value.astype(BF16)
    rest = value - high.astype(F32)
    mid = rest.astype(BF16)
    low = (rest - mid.astype(F32)).astype(BF16)
    return high, mid, low


def state_body(x_ref, b_ref, step_ref, log_ref, out_ref):
    half = pl.program_id(0)
    later = triangle(lambda s, t: s > t)
    logs = log_ref[...]
    suffix = jnp.zeros((HEADS, 1), F32)
    pieces = [None] * NBLK
    for k in reversed(range(NBLK)):
        block = logs[:, k * BLK : (k + 1) * BLK]
        within = jnp.dot(block, later, precision=HIGH, preferred_element_type=F32)
        pieces[k] = within + suffix
        suffix = suffix + jnp.sum(block, axis=1, keepdims=True)
    tail = jnp.exp(jnp.concatenate(pieces, axis=1)) * step_ref[...]
    tail = jnp.concatenate([tail, jnp.zeros((16 - HEADS, TOK), F32)], axis=0)
    tail = jnp.transpose(tail)
    first = half == 0
    scaled = []
    for j in range(HEADS // 2):
        factor = jnp.where(first, tail[:, j : j + 1], tail[:, j + 5 : j + 6])
        part = x_ref[:, j * P_SIZE : (j + 1) * P_SIZE].astype(F32)
        scaled.append((factor * part).astype(BF16))
    scaled = jnp.concatenate(scaled, axis=1)
    state = lax.dot_general(b_ref[...], scaled, TN, preferred_element_type=F32)
    state = state.reshape(16, 8, HALF)
    decay = jnp.exp(suffix)
    rows = lax.broadcasted_iota(jnp.int32, (HEADS, P_SIZE), 0)
    cols = lax.broadcasted_iota(jnp.int32, (HEADS, P_SIZE), 1)
    line = jnp.sum(jnp.where(rows == cols, decay, 0.0), axis=0, keepdims=True)
    high, mid, low = (v.astype(F32) for v in split3(line))
    which = lax.broadcasted_iota(jnp.int32, (8, P_SIZE), 0)
    extra = jnp.where(which == 0, high, jnp.where(which == 1, mid, jnp.where(which == 2, low, 0.0)))
    extra = jnp.broadcast_to(extra[None], (16, 8, P_SIZE))
    out_ref[:, 0] = jnp.concatenate([state, extra], axis=2).astype(BF16)


def shard_state(x, b, step, log_gate):
    return pl.pallas_call(
        state_body,
        grid=(2,),
        in_specs=[
            pl.BlockSpec((TOK, HALF), lambda i: (0, i)),
            pl.BlockSpec((TOK, N), lambda i: (0, 0)),
            pl.BlockSpec((HEADS, TOK), lambda i: (0, 0)),
            pl.BlockSpec((HEADS, TOK), lambda i: (0, 0)),
        ],
        out_specs=pl.BlockSpec((16, 1, 8, HALF + P_SIZE), lambda i: (0, i, 0, 0)),
        out_shape=jax.ShapeDtypeStruct((16, 2, 8, HALF + P_SIZE), BF16),
        compiler_params=pltpu.CompilerParams(vmem_limit_bytes=32 << 20),
        cost_estimate=pl.CostEstimate(flops=2 * TOK * N * CH, bytes_accessed=3 << 20, transcendentals=0),
    )(x, b, step, log_gate)


def scan_body(half_ref, in_ref, out_ref, decay_ref):
    lines = in_ref[:, :, HALF:].astype(F32)
    decay = jnp.sum(lines, axis=1)
    rows = lax.broadcasted_iota(jnp.int32, (P_SIZE, HALF), 0)
    cols = lax.broadcasted_iota(jnp.int32, (P_SIZE, HALF), 1)
    spread = jnp.where(rows == cols // P_SIZE + 5 * half_ref[0], 1.0, 0.0).astype(F32)
    decay_ref[...] = jnp.dot(decay, spread, precision=HIGH, preferred_element_type=F32)
    state = jnp.zeros((8, HALF), F32)
    for k in range(SHARDS):
        out_ref[k] = state.astype(BF16)
        state = decay_ref[k : k + 1, :] * state + in_ref[k, :, :HALF].astype(F32)


def scan_shards(half, received):
    return pl.pallas_call(
        scan_body,
        in_specs=[
            pl.BlockSpec(memory_space=pltpu.SMEM),
            pl.BlockSpec(memory_space=pltpu.VMEM),
        ],
        out_specs=pl.BlockSpec(memory_space=pltpu.VMEM),
        out_shape=jax.ShapeDtypeStruct((SHARDS, 8, HALF), BF16),
        scratch_shapes=[pltpu.VMEM((SHARDS, HALF), F32)],
    )(half, received)


def inner_body(x_ref, g_ref, b_ref, c_ref, step_ref, log_ref, skip_ref, pre_ref, gain_ref, state_ref, past_ref):
    k = pl.program_id(0)

    @pl.when(k == 0)
    def _():
        state_ref[...] = jnp.zeros_like(state_ref)
        past_ref[...] = jnp.zeros_like(past_ref)

    logs = log_ref[...]
    steps = step_ref[...]
    upto = triangle(lambda s, t: s <= t)
    running = jnp.dot(logs, upto, precision=HIGH, preferred_element_type=F32)
    total = running[:, BLK - 1 :]
    tail = jnp.exp(total - running) * steps
    pad = jnp.zeros((16 - HEADS, BLK), F32)
    columns = jnp.transpose(jnp.concatenate([running, pad, tail, pad], axis=0))
    past = past_ref[...][:HEADS, :1]
    since = jnp.transpose(jnp.concatenate([jnp.exp(running + past), pad], axis=0))
    b_rows, c_rows = b_ref[...], c_ref[...]
    scores = lax.dot_general(c_rows, b_rows, NT, preferred_element_type=F32)
    rows = lax.broadcasted_iota(jnp.int32, (BLK, BLK), 0)
    cols = lax.broadcasted_iota(jnp.int32, (BLK, BLK), 1)
    causal = rows >= cols
    scores = jnp.where(causal, scores, 0.0)
    grow = jnp.exp(total)
    carried = jnp.dot(c_rows, state_ref[...].astype(BF16), preferred_element_type=F32)
    scaled = []
    for h in range(HEADS):
        here = slice(h * P_SIZE, (h + 1) * P_SIZE)
        run_col = columns[:, h : h + 1]
        span = run_col - running[h : h + 1, :]
        decays = jnp.exp(jnp.where(causal, span, 0.0))
        weight = (decays * scores * steps[h : h + 1, :]).astype(BF16)
        x_here = x_ref[:, here]
        x_wide = x_here.astype(F32)
        out = jnp.dot(weight, x_here, preferred_element_type=F32)
        out = out + jnp.exp(run_col) * carried[:, here] + skip_ref[0, h] * x_wide
        gate = g_ref[:, here].astype(F32)
        silu = gate / (1.0 + jnp.exp(-gate))
        pre_ref[:, here] = out * silu
        gain_ref[:, here] = (silu * since[:, h : h + 1]).astype(BF16)
        scaled.append((columns[:, 16 + h : 17 + h] * x_wide).astype(BF16))
    added = lax.dot_general(b_rows, jnp.concatenate(scaled, axis=1), TN, preferred_element_type=F32)
    for h in range(HEADS):
        here = slice(h * P_SIZE, (h + 1) * P_SIZE)
        state_ref[:, here] = grow[h : h + 1, :] * state_ref[:, here] + added[:, here]
    past_ref[:HEADS, :] = past_ref[:HEADS, :] + total


def inner(x, g, b, c, step, log_gate, skip):
    return pl.pallas_call(
        inner_body,
        grid=(NBLK,),
        in_specs=[
            pl.BlockSpec((BLK, CH), lambda i: (i, 0)),
            pl.BlockSpec((BLK, CH), lambda i: (i, 0)),
            pl.BlockSpec((BLK, N), lambda i: (i, 0)),
            pl.BlockSpec((BLK, N), lambda i: (i, 0)),
            pl.BlockSpec((HEADS, BLK), lambda i: (0, i)),
            pl.BlockSpec((HEADS, BLK), lambda i: (0, i)),
            pl.BlockSpec(memory_space=pltpu.SMEM),
        ],
        out_specs=[
            pl.BlockSpec((BLK, CH), lambda i: (i, 0)),
            pl.BlockSpec((BLK, CH), lambda i: (i, 0)),
        ],
        out_shape=[
            jax.ShapeDtypeStruct((TOK, CH), F32),
            jax.ShapeDtypeStruct((TOK, CH), BF16),
        ],
        scratch_shapes=[pltpu.VMEM((N, CH), F32), pltpu.VMEM((16, BLK), F32)],
        compiler_params=pltpu.CompilerParams(vmem_limit_bytes=32 << 20),
        cost_estimate=pl.CostEstimate(flops=10 * TOK * N * CH, bytes_accessed=10 << 20, transcendentals=3 * TOK * CH),
    )(x, g, b, c, step, log_gate, skip.reshape(1, HEADS))


def hidden_body(c_ref, in_ref, pre_ref, gain_ref, out_ref):
    c_rows = c_ref[...]
    for half in range(2):
        here = slice(half * HALF, (half + 1) * HALF)
        state = in_ref[:, half].astype(F32).reshape(N, HALF).astype(BF16)
        carried = jnp.dot(c_rows, state, preferred_element_type=F32)
        out_ref[:, here] = (pre_ref[:, here] + gain_ref[:, here].astype(F32) * carried).astype(BF16)


def hidden_of(c, entering, pre, gain):
    return pl.pallas_call(
        hidden_body,
        grid=(3,),
        in_specs=[
            pl.BlockSpec((256, N), lambda i: (i, 0)),
            pl.BlockSpec((16, 2, 8, HALF), lambda i: (0, 0, 0, 0)),
            pl.BlockSpec((256, CH), lambda i: (i, 0)),
            pl.BlockSpec((256, CH), lambda i: (i, 0)),
        ],
        out_specs=pl.BlockSpec((256, CH), lambda i: (i, 0)),
        out_shape=jax.ShapeDtypeStruct((TOK, CH), BF16),
        compiler_params=pltpu.CompilerParams(vmem_limit_bytes=32 << 20),
        cost_estimate=pl.CostEstimate(flops=2 * TOK * N * CH, bytes_accessed=8 << 20, transcendentals=0),
    )(c, entering, pre, gain)


def shift(value, axis, by):
    size = lax.axis_size(axis)
    return lax.ppermute(value, axis, [(i, (i + by) % size) for i in range(size)])


def summed_over_head(hidden, weights):
    groups = lax.axis_size("head")
    mine = lax.axis_index("head")
    width = weights.shape[0] // groups

    def part(group, half):
        start = lax.rem(mine + group + groups, groups) * width + half * (width // 2)
        rows = lax.dynamic_slice_in_dim(weights, start, width // 2, 0)
        return lax.dot_general(hidden, rows, NT, preferred_element_type=F32)

    far = groups // 2
    first = [(1, 0, far), (-1, 1, far)]
    second = [(1, 1, far - 1), (-1, 0, far - 1)]
    flying = {}
    for hop in range(far, 0, -1):
        for streams in (first, second):
            for way, half, start in streams:
                if hop > start:
                    continue
                value = part(way * hop, half)
                if hop < start:
                    value = value + flying[way, half].astype(F32)
                flying[way, half] = shift(value.astype(BF16), "head", way)
    halves = [part(0, half) + flying[1, half].astype(F32) + flying[-1, half].astype(F32) for half in range(2)]
    return jnp.concatenate(halves, axis=1).astype(BF16)


def shards(x, g, b, c, step, log_gate, skip, out_weight):
    weights = lax.all_gather(out_weight, ("seq", "row"), axis=0, tiled=True)
    payload = shard_state(x, b, step, log_gate).reshape(SHARDS, 8, HALF + P_SIZE)
    received = lax.all_to_all(payload, ("seq", "row"), 0, 0)
    pre, gain = inner(x, g, b, c, step, log_gate, skip)
    half = lax.rem(lax.axis_index("row"), 2).reshape(1)
    entering = lax.all_to_all(scan_shards(half, received), ("seq", "row"), 0, 0)
    hidden = hidden_of(c, entering.reshape(16, 2, 8, HALF), pre, gain)
    return summed_over_head(hidden, weights)


def solution(mesh):
    return jax.shard_map(
        shards,
        mesh=mesh,
        in_specs=(
            P(("seq", "row"), "head"),
            P(("seq", "row"), "head"),
            P(("seq", "row"), None),
            P(("seq", "row"), None),
            P("head", ("seq", "row")),
            P("head", ("seq", "row")),
            P("head"),
            P(("seq", "row"), "head"),
        ),
        out_specs=P(("seq", "row"), "head"),
        check_vma=False,
    )
```

```python
import functools

import jax
import jax.numpy as jnp
from jax import lax
from jax.experimental import pallas as pl
from jax.experimental.pallas import tpu as pltpu
from jax.sharding import PartitionSpec as P

P_SIZE = 128
N = 128
BLK = 128
TOK = 768
HEADS = 10
CH = HEADS * P_SIZE
HALF = CH // 2
SHARDS = 32
ROWS = 80
PIECE = 160
NBLK = TOK // BLK
F32 = jnp.float32
BF16 = jnp.bfloat16
HIGH = lax.Precision.HIGHEST
IN_VMEM = pl.BlockSpec(memory_space=pltpu.VMEM)
IN_SMEM = pl.BlockSpec(memory_space=pltpu.SMEM)
ANYWHERE = pl.BlockSpec(memory_space=pl.ANY)
SMALL = pltpu.CompilerParams(vmem_limit_bytes=24 << 20)
NT = (((1,), (1,)), ((), ()))
TN = (((0,), (0,)), ((), ()))


def in_vmem(value):
    return pltpu.with_memory_space_constraint(value, pltpu.VMEM)


def in_hbm(value):
    return pltpu.with_memory_space_constraint(value, pltpu.HBM)


def triangle(upto):
    rows = lax.broadcasted_iota(jnp.int32, (BLK, BLK), 0)
    cols = lax.broadcasted_iota(jnp.int32, (BLK, BLK), 1)
    return jnp.where(upto(rows, cols), 1.0, 0.0).astype(F32)


def split3(value):
    high = value.astype(BF16)
    rest = value - high.astype(F32)
    mid = rest.astype(BF16)
    low = (rest - mid.astype(F32)).astype(BF16)
    return high, mid, low


def state_body(x_ref, b_ref, step_ref, log_ref, out_ref, tail_ref, decay_ref, turned_ref):
    half = pl.program_id(0)

    @pl.when(half == 0)
    def _():
        pad = jnp.zeros((16 - HEADS, BLK), F32)
        logs = log_ref[...]
        stacked = jnp.concatenate(
            [v for k in range(NBLK) for v in (logs[:, k * BLK : (k + 1) * BLK], pad)], axis=0
        )
        within = jnp.dot(stacked, triangle(lambda s, t: s > t), precision=HIGH, preferred_element_type=F32)
        sums = jnp.sum(stacked, axis=1, keepdims=True)
        suffix = jnp.zeros((16, 1), F32)
        pieces = [None] * NBLK
        for k in reversed(range(NBLK)):
            pieces[k] = within[16 * k : 16 * (k + 1)] + suffix
            suffix = suffix + sums[16 * k : 16 * (k + 1)]
        tail_ref[...] = jnp.exp(jnp.concatenate(pieces, axis=1)[:HEADS]) * step_ref[...]
        turned_ref[...] = jnp.transpose(b_ref[...].astype(F32))
        decay_ref[...] = jnp.broadcast_to(jnp.exp(suffix), (16, P_SIZE))

    turned = turned_ref[...]
    parts = []
    for j in range(HEADS // 2):
        row = tail_ref[pl.ds(half * (HEADS // 2) + j, 1), :]
        scaled = (turned * row).astype(BF16)
        here = slice(j * P_SIZE, (j + 1) * P_SIZE)
        parts.append(jnp.dot(scaled, x_ref[:, here], preferred_element_type=F32))
    state = jnp.concatenate(parts, axis=1).reshape(16, 8, HALF)
    rows = lax.broadcasted_iota(jnp.int32, (16, P_SIZE), 0)
    cols = lax.broadcasted_iota(jnp.int32, (16, P_SIZE), 1)
    line = jnp.sum(jnp.where(rows == cols, decay_ref[...], 0.0), axis=0, keepdims=True)
    high, mid, low = (v.astype(F32) for v in split3(line))
    which = lax.broadcasted_iota(jnp.int32, (8, P_SIZE), 0)
    extra = jnp.where(which == 0, high, jnp.where(which == 1, mid, jnp.where(which == 2, low, 0.0)))
    extra = jnp.broadcast_to(extra[None], (16, 8, P_SIZE))
    out_ref[:, 0] = jnp.concatenate([state, extra], axis=2).astype(BF16)


def shard_state(x, b, step, log_gate):
    return pl.pallas_call(
        state_body,
        grid=(2,),
        in_specs=[
            pl.BlockSpec((TOK, HALF), lambda i: (0, i)),
            pl.BlockSpec((TOK, N), lambda i: (0, 0)),
            pl.BlockSpec((HEADS, TOK), lambda i: (0, 0)),
            pl.BlockSpec((HEADS, TOK), lambda i: (0, 0)),
        ],
        out_specs=pl.BlockSpec((16, 1, 8, HALF + P_SIZE), lambda i: (0, i, 0, 0)),
        out_shape=jax.ShapeDtypeStruct((16, 2, 8, HALF + P_SIZE), BF16),
        scratch_shapes=[pltpu.VMEM((HEADS, TOK), F32), pltpu.VMEM((16, P_SIZE), F32), pltpu.VMEM((N, TOK), F32)],
        compiler_params=SMALL,
        cost_estimate=pl.CostEstimate(flops=2 * TOK * N * CH, bytes_accessed=3 << 20, transcendentals=0),
    )(*[in_hbm(v) for v in (x, b, step, log_gate)])


def scan_body(half_ref, in_ref, out_ref, decay_ref):
    lines = in_ref[:, :, HALF:].astype(F32)
    decay = jnp.sum(lines, axis=1)
    rows = lax.broadcasted_iota(jnp.int32, (P_SIZE, HALF), 0)
    cols = lax.broadcasted_iota(jnp.int32, (P_SIZE, HALF), 1)
    spread = jnp.where(rows == cols // P_SIZE + 5 * half_ref[0], 1.0, 0.0).astype(F32)
    decay_ref[...] = jnp.dot(decay, spread, precision=HIGH, preferred_element_type=F32)
    state = jnp.zeros((8, HALF), F32)
    for k in range(SHARDS):
        out_ref[k] = state.astype(BF16)
        state = decay_ref[k : k + 1, :] * state + in_ref[k, :, :HALF].astype(F32)


def scan_shards(half, received):
    return pl.pallas_call(
        scan_body,
        in_specs=[
            pl.BlockSpec(memory_space=pltpu.SMEM),
            pl.BlockSpec(memory_space=pltpu.VMEM),
        ],
        out_specs=pl.BlockSpec(memory_space=pltpu.VMEM),
        out_shape=jax.ShapeDtypeStruct((SHARDS, 8, HALF), BF16),
        scratch_shapes=[pltpu.VMEM((SHARDS, HALF), F32)],
        compiler_params=SMALL,
    )(half, received)


def inner_body(x_ref, g_ref, b_ref, c_ref, step_ref, log_ref, skip_ref, start_ref, before_ref, pre_ref, gain_ref, keep_ref, state_ref, past_ref):
    k = pl.program_id(0)
    tokens = pl.ds(pl.multiple_of(k * BLK, BLK), BLK)

    @pl.when(k == 0)
    def _():
        state_ref[...] = start_ref[...]
        past_ref[...] = before_ref[...]

    keep_ref[tokens, :] = c_ref[...]
    logs = log_ref[...]
    steps = step_ref[...]
    upto = triangle(lambda s, t: s <= t)
    running = jnp.dot(logs, upto, precision=HIGH, preferred_element_type=F32)
    total = running[:, BLK - 1 :]
    tail = jnp.exp(total - running) * steps
    past = past_ref[...][:HEADS, :]
    pad = jnp.zeros((16 - HEADS, BLK), F32)
    columns = jnp.transpose(
        jnp.concatenate([running, pad, jnp.exp(running), pad, jnp.exp(running + past), pad], axis=0)
    )
    b_rows, c_rows = b_ref[...], c_ref[...]
    turned = jnp.transpose(b_rows.astype(F32))
    c_wide = c_rows.astype(F32)
    scores = lax.dot_general(c_rows, b_rows, NT, preferred_element_type=F32)
    rows = lax.broadcasted_iota(jnp.int32, (BLK, BLK), 0)
    cols = lax.broadcasted_iota(jnp.int32, (BLK, BLK), 1)
    causal = rows >= cols
    scores = jnp.where(causal, scores, 0.0)
    grow = jnp.exp(total)
    for h in range(HEADS):
        here = slice(h * P_SIZE, (h + 1) * P_SIZE)
        span = columns[:, h : h + 1] - running[h : h + 1, :]
        decays = jnp.exp(jnp.where(causal, span, 0.0))
        weight = (decays * scores * steps[h : h + 1, :]).astype(BF16)
        reach = (columns[:, 16 + h : 17 + h] * c_wide).astype(BF16)
        x_here = x_ref[:, here]
        state = state_ref[:, here]
        out = jnp.dot(
            jnp.concatenate([weight, reach], axis=1),
            jnp.concatenate([x_here, state.astype(BF16)], axis=0),
            preferred_element_type=F32,
        )
        out = out + skip_ref[0, h] * x_here.astype(F32)
        gate = g_ref[:, here].astype(F32)
        silu = 0.5 * gate * (1.0 + jnp.tanh(0.5 * gate))
        pre_ref[tokens, here] = out * silu
        gain_ref[tokens, here] = (silu * columns[:, 32 + h : 33 + h]).astype(BF16)
        scaled = (turned * tail[h : h + 1, :]).astype(BF16)
        state_ref[:, here] = grow[h : h + 1, :] * state + jnp.dot(scaled, x_here, preferred_element_type=F32)
    past_ref[:HEADS, :] = past_ref[:HEADS, :] + total


def inner(x, g, b, c, step, log_gate, skip, first, state, past):
    count = NBLK // 2
    rows = count * BLK
    return pl.pallas_call(
        inner_body,
        grid=(count,),
        in_specs=[
            pl.BlockSpec((BLK, CH), lambda i: (i + first, 0)),
            pl.BlockSpec((BLK, CH), lambda i: (i + first, 0)),
            pl.BlockSpec((BLK, N), lambda i: (i + first, 0)),
            pl.BlockSpec((BLK, N), lambda i: (i + first, 0)),
            pl.BlockSpec((HEADS, BLK), lambda i: (0, i + first)),
            pl.BlockSpec((HEADS, BLK), lambda i: (0, i + first)),
            IN_SMEM,
            IN_VMEM,
            IN_VMEM,
        ],
        out_specs=[IN_VMEM] * 5,
        out_shape=[
            pltpu.VMEM((rows, CH), F32),
            pltpu.VMEM((rows, CH), BF16),
            pltpu.VMEM((rows, N), BF16),
            jax.ShapeDtypeStruct((N, CH), F32),
            jax.ShapeDtypeStruct((16, BLK), F32),
        ],
        compiler_params=SMALL,
        cost_estimate=pl.CostEstimate(flops=1 << 20, bytes_accessed=1 << 20, transcendentals=0),
    )(*[in_hbm(v) for v in (x, g, b, c, step, log_gate)], skip.reshape(1, HEADS), state, past)


def fetch(table, refs, held, sems, chunks):
    for slot, chunk in enumerate(chunks):
        for j in range(4):
            array = table[8 * chunk + 2 * j]
            block = table[8 * chunk + 2 * j + 1]
            for k, ref in enumerate(refs):

                @pl.when(array == k)
                def _(ref=ref, block=block, slot=slot, j=j):
                    pltpu.make_async_copy(ref.at[block], held.at[slot, j], sems.at[slot, j]).start()


def arrive(refs, held, sems):
    for slot in range(held.shape[0]):
        for j in range(4):
            pltpu.make_async_copy(refs[0].at[0], held.at[slot, j], sems.at[slot, j]).wait()


def product(held, slot, hidden):
    rows = held[slot].reshape(4 * ROWS, CH)
    return lax.dot_general(rows, hidden, NT, preferred_element_type=F32).astype(BF16)


def held_weights(count):
    return pltpu.VMEM((count, 4, ROWS, CH), BF16)


def first_body(table, in_ref, *refs):
    parts, refs, (hidden_ref, up_ref, down_ref, later, held, sems, later_sems) = refs[:6], refs[6:14], refs[14:]
    rows = TOK // 2
    fetch(table, refs, held, sems, (0,))
    fetch(table, refs, later, later_sems, (1, 2))
    states = [in_ref[:, half].astype(F32).reshape(N, HALF).astype(BF16) for half in range(2)]
    for i in range(2):
        here = slice(i * rows, (i + 1) * rows)
        pre_ref, gain_ref, c_ref = parts[3 * i : 3 * i + 3]
        for half in range(2):
            cols = slice(half * HALF, (half + 1) * HALF)
            carried = jnp.dot(c_ref[...], states[half], preferred_element_type=F32)
            hidden_ref[here, cols] = (pre_ref[:, cols] + gain_ref[:, cols].astype(F32) * carried).astype(BF16)
        if i == 0:
            arrive(refs, held, sems)
        out = product(held, 0, hidden_ref[here, :])
        up_ref[:, here] = out[:PIECE]
        down_ref[:, here] = out[PIECE:]
    arrive(refs, later, later_sems)


def first_parts(table, entering, parts, blocks):
    return pl.pallas_call(
        first_body,
        in_specs=[IN_SMEM] + [IN_VMEM] * 7 + [ANYWHERE] * 8,
        out_specs=[IN_VMEM] * 4,
        out_shape=[pltpu.VMEM((TOK, CH), BF16)] + [jax.ShapeDtypeStruct((PIECE, TOK), BF16)] * 2 + [held_weights(2)],
        scratch_shapes=[held_weights(1), pltpu.SemaphoreType.DMA((1, 4)), pltpu.SemaphoreType.DMA((2, 4))],
        compiler_params=SMALL,
        cost_estimate=pl.CostEstimate(flops=2 * 320 * TOK * CH, bytes_accessed=2 << 20, transcendentals=0),
    )(table, entering, *[in_vmem(v) for v in parts], *[in_hbm(v) for v in blocks])


def near_body(chunks, table, hidden_ref, held, *refs):
    refs, (up_ref, down_ref, keep_ref, later, sems) = refs[:8], refs[8:]
    fetch(table, refs, later, sems, chunks)
    out = product(held, 0, hidden_ref[...])
    up_ref[...] = out[PIECE:]
    keep_ref[0] = out[:PIECE]
    out = product(held, 1, hidden_ref[...])
    down_ref[...] = out[:PIECE]
    keep_ref[1] = out[PIECE:]
    arrive(refs, later, sems)


def near_parts(table, hidden, held, blocks, chunks):
    return pl.pallas_call(
        functools.partial(near_body, chunks),
        in_specs=[IN_SMEM, IN_VMEM, IN_VMEM] + [ANYWHERE] * 8,
        out_specs=[IN_VMEM] * 4,
        out_shape=[jax.ShapeDtypeStruct((PIECE, TOK), BF16)] * 2
        + [jax.ShapeDtypeStruct((2, PIECE, TOK), BF16), held_weights(len(chunks))],
        scratch_shapes=[pltpu.SemaphoreType.DMA((len(chunks), 4))],
        compiler_params=SMALL,
        cost_estimate=pl.CostEstimate(flops=4 * 320 * TOK * CH, bytes_accessed=2 << 20, transcendentals=0),
    )(table, in_vmem(hidden), in_vmem(held), *[in_hbm(v) for v in blocks])


def rest_body(chunks, table, hidden_ref, held, *refs):
    refs, (out_ref, *scratch) = refs[:8], refs[8:]
    if chunks:
        later, sems = scratch
        fetch(table, refs, later, sems, chunks)
    for slot in range(held.shape[0]):
        out_ref[slot] = product(held, slot, hidden_ref[...]).reshape(2, PIECE, TOK)
    if chunks:
        arrive(refs, later, sems)


def rest_parts(table, hidden, held, blocks, chunks):
    count, later = held.shape[0], len(chunks)
    return pl.pallas_call(
        functools.partial(rest_body, chunks),
        in_specs=[IN_SMEM, IN_VMEM, IN_VMEM] + [ANYWHERE] * 8,
        out_specs=[IN_VMEM] * (2 if later else 1),
        out_shape=[jax.ShapeDtypeStruct((count, 2, PIECE, TOK), BF16)] + ([held_weights(later)] if later else []),
        scratch_shapes=[pltpu.SemaphoreType.DMA((later, 4))] if later else [],
        compiler_params=SMALL,
        cost_estimate=pl.CostEstimate(flops=2 * count * 320 * TOK * CH, bytes_accessed=count << 20, transcendentals=0),
    )(table, in_vmem(hidden), in_vmem(held), *[in_hbm(v) for v in blocks])


def shift(value, axis, by):
    size = lax.axis_size(axis)
    return lax.ppermute(value, axis, [(i, (i + by) % size) for i in range(size)])


def after(value, earlier):
    return lax.optimization_barrier((value, earlier))[0]


def add(a, b):
    return (a.astype(F32) + b.astype(F32)).astype(BF16)


def place(seq, y, x):
    return seq * 16 + y * 4 + x


def from_line(value, stage, offset):
    pairs = []
    for seq in range(2):
        for y in range(4):
            for x in range(4):
                if (seq == 0) == (stage == 0):
                    source = place(seq, y, (x + offset) % 4)
                else:
                    source = place(seq, (y + offset) % 4, x)
                pairs.append((source, place(seq, y, x)))
    return lax.ppermute(value, ("seq", "row"), pairs)


def line_body(own, one, two, three, out):
    for k, part in enumerate((own, one, two, three)):
        out[k] = part[...]


def line_of(*parts):
    return pl.pallas_call(
        line_body,
        in_specs=[IN_VMEM] * 4,
        out_specs=IN_VMEM,
        out_shape=pltpu.HBM((4, ROWS, CH), BF16),
        compiler_params=SMALL,
    )(*parts)


def weight_table(order):
    seq, row, head = (lax.axis_index(name) for name in ("seq", "row", "head"))
    group = lax.rem(head + jnp.array(order, jnp.int32) + 8, 8)[:, None]
    source = group // 4
    right = lax.rem(jnp.arange(4, dtype=jnp.int32)[None, :] - lax.rem(row, 4) + 4, 4)
    down = lax.rem(group % 4 - row // 4 + 4, 4)
    down, right = jnp.broadcast_arrays(down, right)
    array = jnp.where(source == seq, 0, 4) + jnp.where(source == 0, down, right)
    block = jnp.where(source == 0, right, down)
    return jnp.stack([array, block], axis=2).astype(jnp.int32).reshape(-1)


def projected(entering, parts, blocks):
    table = weight_table((4, 3, -3, 2, -2, 1, -1, 0))
    hidden, ua, db, held = first_parts(table, entering, parts, blocks)
    ua, db = shift(ua, "head", 1), shift(db, "head", -1)
    ub, da, keep, held = near_parts(table, hidden, held, blocks, (3, 4))
    ub, da = shift(ub, "head", 1), shift(da, "head", -1)
    two, held = rest_parts(table, hidden, held, blocks, (5, 6, 7))
    sent = add(keep[0], after(ua, two))
    ua = shift(sent, "head", 1)
    sent = add(keep[1], after(db, sent))
    db = shift(sent, "head", -1)
    (one,) = rest_parts(table, after(hidden, sent), held, blocks, ())
    sent = add(two[0, 1], after(ub, one))
    ub = shift(sent, "head", 1)
    sent = add(two[1, 0], after(da, sent))
    da = shift(sent, "head", -1)
    sent = add(two[0, 0], after(ua, sent))
    ua = shift(sent, "head", 1)
    sent = add(two[1, 1], after(db, sent))
    db = shift(sent, "head", -1)
    sent = add(one[0, 1], after(ub, sent))
    ub = shift(sent, "head", 1)
    sent = add(one[1, 0], after(da, sent))
    da = shift(sent, "head", -1)
    sent = add(one[0, 0], after(ua, sent))
    ua = shift(sent, "head", 1)
    sent = add(one[1, 1], after(db, sent))
    db = shift(sent, "head", -1)
    up = jnp.concatenate([ua, ub]).astype(F32)
    down = jnp.concatenate([da, db]).astype(F32)
    return (one[2].reshape(2 * PIECE, TOK).astype(F32) + up + down).T.astype(BF16)


def shards(x, g, b, c, step, log_gate, skip, out_weight):
    near = [from_line(out_weight, 0, offset) for offset in (1, 2, 3)]
    payload = shard_state(x, b, step, log_gate).reshape(SHARDS, 8, HALF + P_SIZE)
    payload, near = lax.optimization_barrier((payload, near))
    received = lax.all_to_all(payload, ("seq", "row"), 0, 0)
    nothing = (jnp.zeros((N, CH), F32), jnp.zeros((16, BLK), F32))
    *early, state, past = inner(after(x, payload), g, b, c, step, log_gate, skip, 0, *nothing)
    line = line_of(out_weight, *near)
    one, two, three = (from_line(line, 1, offset) for offset in (1, 2, 3))
    half = lax.rem(lax.axis_index("row"), 2).reshape(1)
    slices = scan_shards(half, after(received, past))
    entering = lax.all_to_all(slices, ("seq", "row"), 0, 0)
    *late, _, past = inner(after(x, slices), g, b, c, step, log_gate, skip, NBLK // 2, state, past)
    mine = [line, one, two, three]
    other = [shift(v, "seq", 1) for v in [line] + after(mine[1:], past)]
    return projected(entering.reshape(16, 2, 8, HALF), early + late, mine + other)


def solution(mesh):
    return jax.shard_map(
        shards,
        mesh=mesh,
        in_specs=(
            P(("seq", "row"), "head"),
            P(("seq", "row"), "head"),
            P(("seq", "row"), None),
            P(("seq", "row"), None),
            P("head", ("seq", "row")),
            P("head", ("seq", "row")),
            P("head"),
            P(("seq", "row"), "head"),
        ),
        out_specs=P(("seq", "row"), "head"),
        check_vma=False,
    )
```

```python
import functools

import jax
import jax.numpy as jnp
from jax import lax
from jax.experimental import pallas as pl
from jax.experimental.pallas import tpu as pltpu
from jax.sharding import PartitionSpec as P

P_SIZE = 128
N = 128
BLK = 128
TOK = 768
HEADS = 10
CH = HEADS * P_SIZE
HALF = CH // 2
SHARDS = 32
ROWS = 80
PIECE = 160
FAR, NEAR, NEXT, REST = (4,), (3, -3), (2, -2), (1, -1, 0)
NBLK = TOK // BLK
F32 = jnp.float32
BF16 = jnp.bfloat16
HIGH = lax.Precision.HIGHEST
IN_VMEM = pl.BlockSpec(memory_space=pltpu.VMEM)
IN_SMEM = pl.BlockSpec(memory_space=pltpu.SMEM)
ANYWHERE = pl.BlockSpec(memory_space=pl.ANY)
SMALL = pltpu.CompilerParams(vmem_limit_bytes=24 << 20)
NT = (((1,), (1,)), ((), ()))
TN = (((0,), (0,)), ((), ()))


def in_vmem(value):
    return pltpu.with_memory_space_constraint(value, pltpu.VMEM)


def in_hbm(value):
    return pltpu.with_memory_space_constraint(value, pltpu.HBM)


def triangle(upto):
    rows = lax.broadcasted_iota(jnp.int32, (BLK, BLK), 0)
    cols = lax.broadcasted_iota(jnp.int32, (BLK, BLK), 1)
    return jnp.where(upto(rows, cols), 1.0, 0.0).astype(F32)


def columns_of():
    return lax.rem(lax.axis_index("row"), 4)


def rows_of():
    return lax.axis_index("row") // 4


def split3(value):
    high = value.astype(BF16)
    rest = value - high.astype(F32)
    mid = rest.astype(BF16)
    low = (rest - mid.astype(F32)).astype(BF16)
    return high, mid, low


def state_body(x_ref, b_ref, step_ref, log_ref, out_ref, tail_ref, decay_ref, turned_ref):
    half = pl.program_id(0)

    @pl.when(half == 0)
    def _():
        pad = jnp.zeros((16 - HEADS, BLK), F32)
        logs = log_ref[...]
        stacked = jnp.concatenate(
            [v for k in range(NBLK) for v in (logs[:, k * BLK : (k + 1) * BLK], pad)], axis=0
        )
        within = jnp.dot(stacked, triangle(lambda s, t: s > t), precision=HIGH, preferred_element_type=F32)
        sums = jnp.sum(stacked, axis=1, keepdims=True)
        suffix = jnp.zeros((16, 1), F32)
        pieces = [None] * NBLK
        for k in reversed(range(NBLK)):
            pieces[k] = within[16 * k : 16 * (k + 1)] + suffix
            suffix = suffix + sums[16 * k : 16 * (k + 1)]
        tail_ref[...] = jnp.exp(jnp.concatenate(pieces, axis=1)[:HEADS]) * step_ref[...]
        turned_ref[...] = jnp.transpose(b_ref[...].astype(F32))
        decay_ref[...] = jnp.broadcast_to(jnp.exp(suffix), (16, P_SIZE))

    turned = turned_ref[...]
    parts = []
    for j in range(HEADS // 2):
        row = tail_ref[pl.ds(half * (HEADS // 2) + j, 1), :]
        scaled = (turned * row).astype(BF16)
        here = slice(j * P_SIZE, (j + 1) * P_SIZE)
        parts.append(jnp.dot(scaled, x_ref[:, here], preferred_element_type=F32))
    state = jnp.concatenate(parts, axis=1).reshape(16, 8, HALF)
    rows = lax.broadcasted_iota(jnp.int32, (16, P_SIZE), 0)
    cols = lax.broadcasted_iota(jnp.int32, (16, P_SIZE), 1)
    line = jnp.sum(jnp.where(rows == cols, decay_ref[...], 0.0), axis=0, keepdims=True)
    high, mid, low = (v.astype(F32) for v in split3(line))
    which = lax.broadcasted_iota(jnp.int32, (8, P_SIZE), 0)
    extra = jnp.where(which == 0, high, jnp.where(which == 1, mid, jnp.where(which == 2, low, 0.0)))
    extra = jnp.broadcast_to(extra[None], (16, 8, P_SIZE))
    out_ref[:, 0] = jnp.concatenate([state, extra], axis=2).astype(BF16)


def shard_state(x, b, step, log_gate):
    return pl.pallas_call(
        state_body,
        grid=(2,),
        in_specs=[
            pl.BlockSpec((TOK, HALF), lambda i: (0, i)),
            pl.BlockSpec((TOK, N), lambda i: (0, 0)),
            pl.BlockSpec((HEADS, TOK), lambda i: (0, 0)),
            pl.BlockSpec((HEADS, TOK), lambda i: (0, 0)),
        ],
        out_specs=pl.BlockSpec((16, 1, 8, HALF + P_SIZE), lambda i: (0, i, 0, 0)),
        out_shape=pltpu.HBM((16, 2, 8, HALF + P_SIZE), BF16),
        scratch_shapes=[pltpu.VMEM((HEADS, TOK), F32), pltpu.VMEM((16, P_SIZE), F32), pltpu.VMEM((N, TOK), F32)],
        compiler_params=SMALL,
        cost_estimate=pl.CostEstimate(flops=2 * TOK * N * CH, bytes_accessed=3 << 20, transcendentals=0),
    )(*[in_hbm(v) for v in (x, b, step, log_gate)])


def scan_body(half_ref, in_ref, mark_ref, out_ref, decay_ref):
    lines = in_ref[:, :, HALF:].astype(F32)
    decay = jnp.sum(lines, axis=1)
    rows = lax.broadcasted_iota(jnp.int32, (P_SIZE, HALF), 0)
    cols = lax.broadcasted_iota(jnp.int32, (P_SIZE, HALF), 1)
    spread = jnp.where(rows == cols // P_SIZE + 5 * half_ref[0], 1.0, 0.0).astype(F32)
    decay_ref[...] = jnp.dot(decay, spread, precision=HIGH, preferred_element_type=F32)
    state = jnp.zeros((8, HALF), F32)
    for k in range(SHARDS):
        out_ref[k] = state.astype(BF16)
        state = decay_ref[k : k + 1, :] * state + in_ref[k, :, :HALF].astype(F32)


def scan_shards(half, received, mark):
    return pl.pallas_call(
        scan_body,
        in_specs=[
            IN_SMEM,
            IN_VMEM,
            ANYWHERE,
        ],
        out_specs=IN_VMEM,
        out_shape=pltpu.HBM((SHARDS, 8, HALF), BF16),
        scratch_shapes=[pltpu.VMEM((SHARDS, HALF), F32)],
        compiler_params=SMALL,
    )(half, received, mark)


def inner_body(x_ref, g_ref, b_ref, c_ref, step_ref, log_ref, skip_ref, mark_ref, pre_ref, gain_ref, state_ref, past_ref):
    @pl.when(pl.program_id(0) == 0)
    def _():
        state_ref[...] = jnp.zeros_like(state_ref)
        past_ref[...] = jnp.zeros_like(past_ref)

    logs = log_ref[...]
    steps = step_ref[...]
    upto = triangle(lambda s, t: s <= t)
    running = jnp.dot(logs, upto, precision=HIGH, preferred_element_type=F32)
    total = running[:, BLK - 1 :]
    tail = jnp.exp(total - running) * steps
    past = past_ref[...][:HEADS, :]
    pad = jnp.zeros((16 - HEADS, BLK), F32)
    columns = jnp.transpose(
        jnp.concatenate([running, pad, jnp.exp(running), pad, jnp.exp(running + past), pad], axis=0)
    )
    b_rows, c_rows = b_ref[...], c_ref[...]
    turned = jnp.transpose(b_rows.astype(F32))
    c_wide = c_rows.astype(F32)
    scores = lax.dot_general(c_rows, b_rows, NT, preferred_element_type=F32)
    rows = lax.broadcasted_iota(jnp.int32, (BLK, BLK), 0)
    cols = lax.broadcasted_iota(jnp.int32, (BLK, BLK), 1)
    causal = rows >= cols
    scores = jnp.where(causal, scores, 0.0)
    grow = jnp.exp(total)
    for h in range(HEADS):
        here = slice(h * P_SIZE, (h + 1) * P_SIZE)
        span = columns[:, h : h + 1] - running[h : h + 1, :]
        decays = jnp.exp(jnp.where(causal, span, 0.0))
        weight = (decays * scores * steps[h : h + 1, :]).astype(BF16)
        reach = (columns[:, 16 + h : 17 + h] * c_wide).astype(BF16)
        x_here = x_ref[:, here]
        state = state_ref[:, here]
        out = jnp.dot(
            jnp.concatenate([weight, reach], axis=1),
            jnp.concatenate([x_here, state.astype(BF16)], axis=0),
            preferred_element_type=F32,
        )
        out = out + skip_ref[0, h] * x_here.astype(F32)
        gate = g_ref[:, here].astype(F32)
        silu = 0.5 * gate * (1.0 + jnp.tanh(0.5 * gate))
        pre_ref[:, here] = (out * silu).astype(BF16)
        gain_ref[:, here] = (silu * columns[:, 32 + h : 33 + h]).astype(BF16)
        scaled = (turned * tail[h : h + 1, :]).astype(BF16)
        state_ref[:, here] = grow[h : h + 1, :] * state + jnp.dot(scaled, x_here, preferred_element_type=F32)
    past_ref[:HEADS, :] = past_ref[:HEADS, :] + total


def inner(x, g, b, c, step, log_gate, skip, mark):
    return pl.pallas_call(
        inner_body,
        grid=(NBLK,),
        in_specs=[
            pl.BlockSpec((BLK, CH), lambda i: (i, 0)),
            pl.BlockSpec((BLK, CH), lambda i: (i, 0)),
            pl.BlockSpec((BLK, N), lambda i: (i, 0)),
            pl.BlockSpec((BLK, N), lambda i: (i, 0)),
            pl.BlockSpec((HEADS, BLK), lambda i: (0, i)),
            pl.BlockSpec((HEADS, BLK), lambda i: (0, i)),
            IN_SMEM,
            ANYWHERE,
        ],
        out_specs=[pl.BlockSpec((BLK, CH), lambda i: (i, 0))] * 2,
        out_shape=[pltpu.HBM((TOK, CH), BF16)] * 2,
        scratch_shapes=[pltpu.VMEM((N, CH), F32), pltpu.VMEM((16, BLK), F32)],
        compiler_params=SMALL,
        cost_estimate=pl.CostEstimate(flops=1 << 20, bytes_accessed=40 << 20, transcendentals=0),
    )(*[in_hbm(v) for v in (x, g, b, c, step, log_gate)], skip.reshape(1, HEADS), in_hbm(mark))


def hold_body(*refs):
    pass


def hold(values, *marks):
    count = len(values)
    return pl.pallas_call(
        hold_body,
        in_specs=[ANYWHERE] * (count + len(marks)),
        out_specs=[ANYWHERE] * count,
        out_shape=[pltpu.HBM(v.shape, v.dtype) for v in values],
        input_output_aliases={i: i for i in range(count)},
        compiler_params=SMALL,
        cost_estimate=pl.CostEstimate(flops=0, bytes_accessed=0, transcendentals=0),
    )(*[in_hbm(v) for v in values], *marks)


def fetch(refs, held, sems, ups):
    seq, head = lax.axis_index("seq"), lax.axis_index("head")
    for slot, up in enumerate(ups):
        group = lax.rem(head + (up + 8), 8)
        first = group < 4
        down = lax.rem(lax.rem(group, 4) - rows_of() + 4, 4)
        base = jnp.where((seq == 0) == first, 0, 4)
        for j in range(4):
            right = lax.rem(j - columns_of() + 4, 4)
            array = base + jnp.where(first, down, right)
            block = jnp.where(first, right, down)
            for k, ref in enumerate(refs):

                @pl.when(array == k)
                def _(ref=ref, block=block, slot=slot, j=j):
                    pltpu.make_async_copy(ref.at[block], held.at[slot, j], sems.at[slot, j]).start()


def arrive(refs, held, sems):
    for slot in range(held.shape[0]):
        for j in range(4):
            pltpu.make_async_copy(refs[0].at[0], held.at[slot, j], sems.at[slot, j]).wait()


def product(held, slot, hidden):
    rows = held[slot].reshape(4 * ROWS, CH)
    return lax.dot_general(rows, hidden, NT, preferred_element_type=F32).astype(BF16)


def held_weights(count):
    return pltpu.VMEM((count, 4, ROWS, CH), BF16)


def first_body(in_ref, c_ref, *refs):
    parts, refs = refs[:2], refs[2:]
    refs, (hidden_ref, up_ref, down_ref, later, pre, gain, part_sems, held, sems, later_sems) = refs[:8], refs[8:]
    rows = TOK // 2
    copies = []
    for i in range(2):
        here = pl.ds(i * rows, rows)
        for j, (part, held_part) in enumerate(zip(parts, (pre, gain))):
            copies.append(pltpu.make_async_copy(part.at[here], held_part.at[here], part_sems.at[i, j]))
            copies[-1].start()
        if i == 0:
            fetch(refs, held, sems, FAR)
    fetch(refs, later, later_sems, NEAR)
    states = [in_ref[:, half].astype(F32).reshape(N, HALF).astype(BF16) for half in range(2)]
    for i in range(2):
        here = slice(i * rows, (i + 1) * rows)
        copies[2 * i].wait()
        copies[2 * i + 1].wait()
        for half in range(2):
            cols = slice(half * HALF, (half + 1) * HALF)
            carried = jnp.dot(c_ref[here, :], states[half], preferred_element_type=F32)
            hidden_ref[here, cols] = (pre[here, cols].astype(F32) + gain[here, cols].astype(F32) * carried).astype(BF16)
        if i == 0:
            arrive(refs, held, sems)
        out = product(held, 0, hidden_ref[here, :])
        up_ref[:, here] = out[:PIECE]
        down_ref[:, here] = out[PIECE:]
    arrive(refs, later, later_sems)


def first_parts(entering, c, parts, blocks):
    return pl.pallas_call(
        first_body,
        in_specs=[IN_VMEM] * 2 + [ANYWHERE] * 10,
        out_specs=[IN_VMEM] * 4,
        out_shape=[pltpu.VMEM((TOK, CH), BF16)] + [jax.ShapeDtypeStruct((PIECE, TOK), BF16)] * 2 + [held_weights(2)],
        scratch_shapes=[
            pltpu.VMEM((TOK, CH), BF16),
            pltpu.VMEM((TOK, CH), BF16),
            pltpu.SemaphoreType.DMA((2, 2)),
            held_weights(1),
            pltpu.SemaphoreType.DMA((1, 4)),
            pltpu.SemaphoreType.DMA((2, 4)),
        ],
        compiler_params=SMALL,
        cost_estimate=pl.CostEstimate(flops=2 * 320 * TOK * CH, bytes_accessed=2 << 20, transcendentals=0),
    )(entering, *[in_hbm(v) for v in (c, *parts, *blocks)])


def near_body(ups, hidden_ref, held, *refs):
    refs, (up_ref, down_ref, keep_ref, later, sems) = refs[:8], refs[8:]
    fetch(refs, later, sems, ups)
    out = product(held, 0, hidden_ref[...])
    up_ref[...] = out[PIECE:]
    keep_ref[0] = out[:PIECE]
    out = product(held, 1, hidden_ref[...])
    down_ref[...] = out[:PIECE]
    keep_ref[1] = out[PIECE:]
    arrive(refs, later, sems)


def near_parts(hidden, held, blocks, ups):
    return pl.pallas_call(
        functools.partial(near_body, ups),
        in_specs=[IN_VMEM, IN_VMEM] + [ANYWHERE] * 8,
        out_specs=[IN_VMEM] * 4,
        out_shape=[jax.ShapeDtypeStruct((PIECE, TOK), BF16)] * 2
        + [jax.ShapeDtypeStruct((2, PIECE, TOK), BF16), held_weights(len(ups))],
        scratch_shapes=[pltpu.SemaphoreType.DMA((len(ups), 4))],
        compiler_params=SMALL,
        cost_estimate=pl.CostEstimate(flops=4 * 320 * TOK * CH, bytes_accessed=2 << 20, transcendentals=0),
    )(in_vmem(hidden), in_vmem(held), *[in_hbm(v) for v in blocks])


def rest_body(ups, hidden_ref, held, *refs):
    refs, (out_ref, *scratch) = refs[:8], refs[8:]
    if ups:
        later, sems = scratch
        fetch(refs, later, sems, ups)
    for slot in range(held.shape[0]):
        out_ref[slot] = product(held, slot, hidden_ref[...]).reshape(2, PIECE, TOK)
    if ups:
        arrive(refs, later, sems)


def rest_parts(hidden, held, blocks, ups):
    count, later = held.shape[0], len(ups)
    return pl.pallas_call(
        functools.partial(rest_body, ups),
        in_specs=[IN_VMEM, IN_VMEM] + [ANYWHERE] * 8,
        out_specs=[IN_VMEM] * (2 if later else 1),
        out_shape=[jax.ShapeDtypeStruct((count, 2, PIECE, TOK), BF16)] + ([held_weights(later)] if later else []),
        scratch_shapes=[pltpu.SemaphoreType.DMA((later, 4))] if later else [],
        compiler_params=SMALL,
        cost_estimate=pl.CostEstimate(flops=2 * count * 320 * TOK * CH, bytes_accessed=count << 20, transcendentals=0),
    )(in_vmem(hidden), in_vmem(held), *[in_hbm(v) for v in blocks])


def shift(value, axis, by):
    size = lax.axis_size(axis)
    return lax.ppermute(value, axis, [(i, (i + by) % size) for i in range(size)])


def after(value, earlier):
    return lax.optimization_barrier((value, earlier))[0]


def add(a, b):
    return (a.astype(F32) + b.astype(F32)).astype(BF16)


def place(seq, y, x):
    return seq * 16 + y * 4 + x


def from_line(value, stage, offset):
    pairs = []
    for seq in range(2):
        for y in range(4):
            for x in range(4):
                if (seq == 0) == (stage == 0):
                    source = place(seq, y, (x + offset) % 4)
                else:
                    source = place(seq, (y + offset) % 4, x)
                pairs.append((source, place(seq, y, x)))
    return lax.ppermute(value, ("seq", "row"), pairs)


def line_body(own, one, two, three, mark, out):
    for k, part in enumerate((own, one, two, three)):
        out[k] = part[...]


def line_of(*parts):
    return pl.pallas_call(
        line_body,
        in_specs=[IN_VMEM] * 4 + [ANYWHERE],
        out_specs=IN_VMEM,
        out_shape=pltpu.HBM((4, ROWS, CH), BF16),
        compiler_params=SMALL,
        cost_estimate=pl.CostEstimate(flops=0, bytes_accessed=1 << 10, transcendentals=0),
    )(*parts)


def projected(entering, c, parts, blocks):
    hidden, ua, db, held = first_parts(entering, c, parts, blocks)
    ua, db = shift(ua, "head", 1), shift(db, "head", -1)
    ub, da, keep, held = near_parts(hidden, held, blocks, NEXT)
    ub, da = shift(ub, "head", 1), shift(da, "head", -1)
    two, held = rest_parts(hidden, held, blocks, REST)
    sent = add(keep[0], after(ua, two))
    ua = shift(sent, "head", 1)
    sent = add(keep[1], after(db, sent))
    db = shift(sent, "head", -1)
    (one,) = rest_parts(after(hidden, sent), held, blocks, ())
    sent = add(two[0, 1], after(ub, one))
    ub = shift(sent, "head", 1)
    sent = add(two[1, 0], after(da, sent))
    da = shift(sent, "head", -1)
    sent = add(two[0, 0], after(ua, sent))
    ua = shift(sent, "head", 1)
    sent = add(two[1, 1], after(db, sent))
    db = shift(sent, "head", -1)
    sent = add(one[0, 1], after(ub, sent))
    ub = shift(sent, "head", 1)
    sent = add(one[1, 0], after(da, sent))
    da = shift(sent, "head", -1)
    sent = add(one[0, 0], after(ua, sent))
    ua = shift(sent, "head", 1)
    sent = add(one[1, 1], after(db, sent))
    db = shift(sent, "head", -1)
    up = jnp.concatenate([ua, ub]).astype(F32)
    down = jnp.concatenate([da, db]).astype(F32)
    return (one[2].reshape(2 * PIECE, TOK).astype(F32) + up + down).T.astype(BF16)


def shards(x, g, b, c, step, log_gate, skip, out_weight):
    near = [from_line(out_weight, 0, offset) for offset in (1, 2, 3)]
    payload = shard_state(x, b, step, log_gate)
    line = line_of(out_weight, *near, in_hbm(payload))
    one, three = (from_line(line, 1, offset) for offset in (1, 3))
    received = lax.all_to_all(payload.reshape(SHARDS, 8, HALF + P_SIZE), ("seq", "row"), 0, 0)
    parts = inner(x, g, b, c, step, log_gate, skip, payload)
    line, one, three = hold([line, one, three], received, in_hbm(parts[0]))
    two = from_line(line, 1, 2)
    other = [shift(v, "seq", 1) for v in (line, one, three)]
    half = lax.rem(lax.axis_index("row"), 2).reshape(1)
    slices = scan_shards(half, received, in_hbm(parts[0]))
    entering = lax.all_to_all(slices, ("seq", "row"), 0, 0)
    (two,) = hold([two], entering)
    other.insert(2, shift(two, "seq", 1))
    return projected(entering.reshape(16, 2, 8, HALF), c, parts, [line, one, two, three] + other)


def solution(mesh):
    return jax.shard_map(
        shards,
        mesh=mesh,
        in_specs=(
            P(("seq", "row"), "head"),
            P(("seq", "row"), "head"),
            P(("seq", "row"), None),
            P(("seq", "row"), None),
            P("head", ("seq", "row")),
            P("head", ("seq", "row")),
            P("head"),
            P(("seq", "row"), "head"),
        ),
        out_specs=P(("seq", "row"), "head"),
        check_vma=False,
    )
```

```python
import functools

import jax
import jax.numpy as jnp
from jax import lax
from jax.experimental import pallas as pl
from jax.experimental.pallas import tpu as pltpu
from jax.sharding import PartitionSpec as P

P_SIZE = 128
N = 128
BLK = 128
TOK = 768
HEADS = 10
CH = HEADS * P_SIZE
HALF = CH // 2
SHARDS = 32
ROWS = 80
PIECE = 160
FAR, NEAR, NEXT, REST = (4,), (3, -3), (2, -2), (1, -1, 0)
NBLK = TOK // BLK
F32 = jnp.float32
BF16 = jnp.bfloat16
HIGH = lax.Precision.HIGHEST
IN_VMEM = pl.BlockSpec(memory_space=pltpu.VMEM)
IN_SMEM = pl.BlockSpec(memory_space=pltpu.SMEM)
ANYWHERE = pl.BlockSpec(memory_space=pl.ANY)
SMALL = pltpu.CompilerParams(vmem_limit_bytes=24 << 20)
NT = (((1,), (1,)), ((), ()))
TN = (((0,), (0,)), ((), ()))


def in_vmem(value):
    return pltpu.with_memory_space_constraint(value, pltpu.VMEM)


def in_hbm(value):
    return pltpu.with_memory_space_constraint(value, pltpu.HBM)


def triangle(upto):
    rows = lax.broadcasted_iota(jnp.int32, (BLK, BLK), 0)
    cols = lax.broadcasted_iota(jnp.int32, (BLK, BLK), 1)
    return jnp.where(upto(rows, cols), 1.0, 0.0).astype(F32)


def columns_of():
    return lax.rem(lax.axis_index("row"), 4)


def rows_of():
    return lax.axis_index("row") // 4


def split3(value):
    high = value.astype(BF16)
    rest = value - high.astype(F32)
    mid = rest.astype(BF16)
    low = (rest - mid.astype(F32)).astype(BF16)
    return high, mid, low


def state_body(x_ref, b_ref, step_ref, log_ref, out_ref, tail_ref, decay_ref, turned_ref):
    half = pl.program_id(0)

    @pl.when(half == 0)
    def _():
        pad = jnp.zeros((16 - HEADS, BLK), F32)
        logs = log_ref[...]
        stacked = jnp.concatenate(
            [v for k in range(NBLK) for v in (logs[:, k * BLK : (k + 1) * BLK], pad)], axis=0
        )
        within = jnp.dot(stacked, triangle(lambda s, t: s > t), precision=HIGH, preferred_element_type=F32)
        sums = jnp.sum(stacked, axis=1, keepdims=True)
        suffix = jnp.zeros((16, 1), F32)
        pieces = [None] * NBLK
        for k in reversed(range(NBLK)):
            pieces[k] = within[16 * k : 16 * (k + 1)] + suffix
            suffix = suffix + sums[16 * k : 16 * (k + 1)]
        tail_ref[...] = jnp.exp(jnp.concatenate(pieces, axis=1)[:HEADS]) * step_ref[...]
        turned_ref[...] = jnp.transpose(b_ref[...].astype(F32))
        decay_ref[...] = jnp.broadcast_to(jnp.exp(suffix), (16, P_SIZE))

    turned = turned_ref[...]
    parts = []
    for j in range(HEADS // 2):
        row = tail_ref[pl.ds(half * (HEADS // 2) + j, 1), :]
        scaled = (turned * row).astype(BF16)
        here = slice(j * P_SIZE, (j + 1) * P_SIZE)
        parts.append(jnp.dot(scaled, x_ref[:, here], preferred_element_type=F32))
    state = jnp.concatenate(parts, axis=1).reshape(16, 8, HALF)
    rows = lax.broadcasted_iota(jnp.int32, (16, P_SIZE), 0)
    cols = lax.broadcasted_iota(jnp.int32, (16, P_SIZE), 1)
    line = jnp.sum(jnp.where(rows == cols, decay_ref[...], 0.0), axis=0, keepdims=True)
    high, mid, low = (v.astype(F32) for v in split3(line))
    which = lax.broadcasted_iota(jnp.int32, (8, P_SIZE), 0)
    extra = jnp.where(which == 0, high, jnp.where(which == 1, mid, jnp.where(which == 2, low, 0.0)))
    extra = jnp.broadcast_to(extra[None], (16, 8, P_SIZE))
    out_ref[:, 0] = jnp.concatenate([state, extra], axis=2).astype(BF16)


def shard_state(x, b, step, log_gate):
    return pl.pallas_call(
        state_body,
        grid=(2,),
        in_specs=[
            pl.BlockSpec((TOK, HALF), lambda i: (0, i)),
            pl.BlockSpec((TOK, N), lambda i: (0, 0)),
            pl.BlockSpec((HEADS, TOK), lambda i: (0, 0)),
            pl.BlockSpec((HEADS, TOK), lambda i: (0, 0)),
        ],
        out_specs=pl.BlockSpec((16, 1, 8, HALF + P_SIZE), lambda i: (0, i, 0, 0)),
        out_shape=pltpu.HBM((16, 2, 8, HALF + P_SIZE), BF16),
        scratch_shapes=[pltpu.VMEM((HEADS, TOK), F32), pltpu.VMEM((16, P_SIZE), F32), pltpu.VMEM((N, TOK), F32)],
        compiler_params=SMALL,
        cost_estimate=pl.CostEstimate(flops=2 * TOK * N * CH, bytes_accessed=3 << 20, transcendentals=0),
    )(*[in_hbm(v) for v in (x, b, step, log_gate)])


def scan_body(half_ref, in_ref, mark_ref, out_ref, decay_ref):
    lines = in_ref[:, :, HALF:].astype(F32)
    decay = jnp.sum(lines, axis=1)
    rows = lax.broadcasted_iota(jnp.int32, (P_SIZE, HALF), 0)
    cols = lax.broadcasted_iota(jnp.int32, (P_SIZE, HALF), 1)
    spread = jnp.where(rows == cols // P_SIZE + 5 * half_ref[0], 1.0, 0.0).astype(F32)
    decay_ref[...] = jnp.dot(decay, spread, precision=HIGH, preferred_element_type=F32)
    state = jnp.zeros((8, HALF), F32)
    for k in range(SHARDS):
        out_ref[k] = state.astype(BF16)
        state = decay_ref[k : k + 1, :] * state + in_ref[k, :, :HALF].astype(F32)


def scan_shards(half, received, mark):
    return pl.pallas_call(
        scan_body,
        in_specs=[
            IN_SMEM,
            IN_VMEM,
            ANYWHERE,
        ],
        out_specs=IN_VMEM,
        out_shape=pltpu.HBM((SHARDS, 8, HALF), BF16),
        scratch_shapes=[pltpu.VMEM((SHARDS, HALF), F32)],
        compiler_params=SMALL,
    )(half, received, mark)


def inner_body(x_ref, g_ref, b_ref, c_ref, step_ref, log_ref, skip_ref, mark_ref, pre_ref, gain_ref, state_ref, past_ref):
    @pl.when(pl.program_id(0) == 0)
    def _():
        state_ref[...] = jnp.zeros_like(state_ref)
        past_ref[...] = jnp.zeros_like(past_ref)

    logs = log_ref[...]
    steps = step_ref[...]
    upto = triangle(lambda s, t: s <= t)
    running = jnp.dot(logs, upto, precision=HIGH, preferred_element_type=F32)
    total = running[:, BLK - 1 :]
    tail = jnp.exp(total - running) * steps
    past = past_ref[...][:HEADS, :]
    pad = jnp.zeros((16 - HEADS, BLK), F32)
    columns = jnp.transpose(
        jnp.concatenate([running, pad, jnp.exp(running), pad, jnp.exp(running + past), pad], axis=0)
    )
    b_rows, c_rows = b_ref[...], c_ref[...]
    turned = jnp.transpose(b_rows.astype(F32))
    c_wide = c_rows.astype(F32)
    scores = lax.dot_general(c_rows, b_rows, NT, preferred_element_type=F32)
    rows = lax.broadcasted_iota(jnp.int32, (BLK, BLK), 0)
    cols = lax.broadcasted_iota(jnp.int32, (BLK, BLK), 1)
    causal = rows >= cols
    scores = jnp.where(causal, scores, 0.0)
    grow = jnp.exp(total)
    for h in range(HEADS):
        here = slice(h * P_SIZE, (h + 1) * P_SIZE)
        span = columns[:, h : h + 1] - running[h : h + 1, :]
        decays = jnp.exp(jnp.where(causal, span, 0.0))
        weight = (decays * scores * steps[h : h + 1, :]).astype(BF16)
        reach = (columns[:, 16 + h : 17 + h] * c_wide).astype(BF16)
        x_here = x_ref[:, here]
        state = state_ref[:, here]
        out = jnp.dot(
            jnp.concatenate([weight, reach], axis=1),
            jnp.concatenate([x_here, state.astype(BF16)], axis=0),
            preferred_element_type=F32,
        )
        out = out + skip_ref[0, h] * x_here.astype(F32)
        gate = g_ref[:, here].astype(F32)
        silu = 0.5 * gate * (1.0 + jnp.tanh(0.5 * gate))
        pre_ref[:, here] = (out * silu).astype(BF16)
        gain_ref[:, here] = (silu * columns[:, 32 + h : 33 + h]).astype(BF16)
        scaled = (turned * tail[h : h + 1, :]).astype(BF16)
        state_ref[:, here] = grow[h : h + 1, :] * state + jnp.dot(scaled, x_here, preferred_element_type=F32)
    past_ref[:HEADS, :] = past_ref[:HEADS, :] + total


def inner(x, g, b, c, step, log_gate, skip, mark):
    return pl.pallas_call(
        inner_body,
        grid=(NBLK,),
        in_specs=[
            pl.BlockSpec((BLK, CH), lambda i: (i, 0)),
            pl.BlockSpec((BLK, CH), lambda i: (i, 0)),
            pl.BlockSpec((BLK, N), lambda i: (i, 0)),
            pl.BlockSpec((BLK, N), lambda i: (i, 0)),
            pl.BlockSpec((HEADS, BLK), lambda i: (0, i)),
            pl.BlockSpec((HEADS, BLK), lambda i: (0, i)),
            IN_SMEM,
            ANYWHERE,
        ],
        out_specs=[pl.BlockSpec((BLK, CH), lambda i: (i, 0))] * 2,
        out_shape=[pltpu.HBM((TOK, CH), BF16)] * 2,
        scratch_shapes=[pltpu.VMEM((N, CH), F32), pltpu.VMEM((16, BLK), F32)],
        compiler_params=SMALL,
        cost_estimate=pl.CostEstimate(flops=1 << 20, bytes_accessed=40 << 20, transcendentals=0),
    )(*[in_hbm(v) for v in (x, g, b, c, step, log_gate)], skip.reshape(1, HEADS), in_hbm(mark))


def hold_body(*refs):
    pass


def hold(values, *marks):
    count = len(values)
    return pl.pallas_call(
        hold_body,
        in_specs=[ANYWHERE] * (count + len(marks)),
        out_specs=[ANYWHERE] * count,
        out_shape=[pltpu.HBM(v.shape, v.dtype) for v in values],
        input_output_aliases={i: i for i in range(count)},
        compiler_params=SMALL,
        cost_estimate=pl.CostEstimate(flops=0, bytes_accessed=0, transcendentals=0),
    )(*[in_hbm(v) for v in values], *marks)


def fetch(refs, held, sems, ups):
    seq, head = lax.axis_index("seq"), lax.axis_index("head")
    for slot, up in enumerate(ups):
        group = lax.rem(head + (up + 8), 8)
        first = group < 4
        down = lax.rem(lax.rem(group, 4) - rows_of() + 4, 4)
        base = jnp.where((seq == 0) == first, 0, 4)
        for j in range(4):
            right = lax.rem(j - columns_of() + 4, 4)
            array = base + jnp.where(first, down, right)
            block = jnp.where(first, right, down)
            for k, ref in enumerate(refs):

                @pl.when(array == k)
                def _(ref=ref, block=block, slot=slot, j=j):
                    pltpu.make_async_copy(ref.at[block], held.at[slot, j], sems.at[slot, j]).start()


def arrive(refs, held, sems):
    for slot in range(held.shape[0]):
        for j in range(4):
            pltpu.make_async_copy(refs[0].at[0], held.at[slot, j], sems.at[slot, j]).wait()


def product(held, slot, hidden):
    rows = held[slot].reshape(4 * ROWS, CH)
    return lax.dot_general(rows, hidden, NT, preferred_element_type=F32).astype(BF16)


def held_weights(count):
    return pltpu.VMEM((count, 4, ROWS, CH), BF16)


def hidden_body(in_ref, c_ref, pre_ref, gain_ref, hidden_ref, state_ref):
    rows = c_ref.shape[0]
    here = pl.ds(pl.multiple_of(pl.program_id(0) * rows, rows), rows)

    @pl.when(pl.program_id(0) == 0)
    def _():
        for half in range(2):
            state_ref[half] = in_ref[:, half].astype(F32).reshape(N, HALF).astype(BF16)

    for half in range(2):
        cols = slice(half * HALF, (half + 1) * HALF)
        carried = jnp.dot(c_ref[...], state_ref[half], preferred_element_type=F32)
        hidden_ref[here, cols] = (pre_ref[:, cols].astype(F32) + gain_ref[:, cols].astype(F32) * carried).astype(BF16)


def hidden_of(entering, c, pre, gain):
    rows = 256
    return pl.pallas_call(
        hidden_body,
        grid=(TOK // rows,),
        in_specs=[
            pl.BlockSpec((16, 2, 8, HALF), lambda i: (0, 0, 0, 0)),
            pl.BlockSpec((rows, N), lambda i: (i, 0)),
            pl.BlockSpec((rows, CH), lambda i: (i, 0)),
            pl.BlockSpec((rows, CH), lambda i: (i, 0)),
        ],
        out_specs=IN_VMEM,
        out_shape=pltpu.VMEM((TOK, CH), BF16),
        scratch_shapes=[pltpu.VMEM((2, N, HALF), BF16)],
        compiler_params=SMALL,
        cost_estimate=pl.CostEstimate(flops=2 * TOK * N * CH, bytes_accessed=5 << 20, transcendentals=0),
    )(entering, *[in_hbm(v) for v in (c, pre, gain)])


def in_place(blocks):
    return [v if k == 6 else in_hbm(v) for k, v in enumerate(blocks)]


def far_body(hidden_ref, *refs):
    refs, (up_ref, down_ref, later, held, sems, later_sems) = refs[:8], refs[8:]
    fetch(refs, held, sems, FAR)
    fetch(refs, later, later_sems, NEAR)
    arrive(refs, held, sems)
    out = product(held, 0, hidden_ref[...])
    up_ref[...] = out[:PIECE]
    down_ref[...] = out[PIECE:]
    arrive(refs, later, later_sems)


def far_parts(hidden, blocks):
    return pl.pallas_call(
        far_body,
        in_specs=[IN_VMEM] + [ANYWHERE] * 8,
        out_specs=[IN_VMEM] * 3,
        out_shape=[jax.ShapeDtypeStruct((PIECE, TOK), BF16)] * 2 + [held_weights(2)],
        scratch_shapes=[held_weights(1), pltpu.SemaphoreType.DMA((1, 4)), pltpu.SemaphoreType.DMA((2, 4))],
        compiler_params=SMALL,
        cost_estimate=pl.CostEstimate(flops=2 * 320 * TOK * CH, bytes_accessed=2 << 20, transcendentals=0),
    )(in_vmem(hidden), *in_place(blocks))


def near_body(ups, hidden_ref, held, *refs):
    refs, (up_ref, down_ref, keep_ref, later, sems) = refs[:8], refs[8:]
    fetch(refs, later, sems, ups)
    out = product(held, 0, hidden_ref[...])
    up_ref[...] = out[PIECE:]
    keep_ref[0] = out[:PIECE]
    out = product(held, 1, hidden_ref[...])
    down_ref[...] = out[:PIECE]
    keep_ref[1] = out[PIECE:]
    arrive(refs, later, sems)


def near_parts(hidden, held, blocks, ups):
    return pl.pallas_call(
        functools.partial(near_body, ups),
        in_specs=[IN_VMEM, IN_VMEM] + [ANYWHERE] * 8,
        out_specs=[IN_VMEM] * 4,
        out_shape=[jax.ShapeDtypeStruct((PIECE, TOK), BF16)] * 2
        + [jax.ShapeDtypeStruct((2, PIECE, TOK), BF16), held_weights(len(ups))],
        scratch_shapes=[pltpu.SemaphoreType.DMA((len(ups), 4))],
        compiler_params=SMALL,
        cost_estimate=pl.CostEstimate(flops=4 * 320 * TOK * CH, bytes_accessed=2 << 20, transcendentals=0),
    )(in_vmem(hidden), in_vmem(held), *in_place(blocks))


def rest_body(ups, hidden_ref, held, *refs):
    refs, (out_ref, *scratch) = refs[:8], refs[8:]
    if ups:
        later, sems = scratch
        fetch(refs, later, sems, ups)
    for slot in range(held.shape[0]):
        out_ref[slot] = product(held, slot, hidden_ref[...]).reshape(2, PIECE, TOK)
    if ups:
        arrive(refs, later, sems)


def rest_parts(hidden, held, blocks, ups):
    count, later = held.shape[0], len(ups)
    return pl.pallas_call(
        functools.partial(rest_body, ups),
        in_specs=[IN_VMEM, IN_VMEM] + [ANYWHERE] * 8,
        out_specs=[IN_VMEM] * (2 if later else 1),
        out_shape=[jax.ShapeDtypeStruct((count, 2, PIECE, TOK), BF16)] + ([held_weights(later)] if later else []),
        scratch_shapes=[pltpu.SemaphoreType.DMA((later, 4))] if later else [],
        compiler_params=SMALL,
        cost_estimate=pl.CostEstimate(flops=2 * count * 320 * TOK * CH, bytes_accessed=count << 20, transcendentals=0),
    )(in_vmem(hidden), in_vmem(held), *in_place(blocks))


def shift(value, axis, by):
    size = lax.axis_size(axis)
    return lax.ppermute(value, axis, [(i, (i + by) % size) for i in range(size)])


def after(value, earlier):
    return lax.optimization_barrier((value, earlier))[0]


def add(a, b):
    return (a.astype(F32) + b.astype(F32)).astype(BF16)


def place(seq, y, x):
    return seq * 16 + y * 4 + x


def from_line(value, stage, offset):
    pairs = []
    for seq in range(2):
        for y in range(4):
            for x in range(4):
                if (seq == 0) == (stage == 0):
                    source = place(seq, y, (x + offset) % 4)
                else:
                    source = place(seq, (y + offset) % 4, x)
                pairs.append((source, place(seq, y, x)))
    return lax.ppermute(value, ("seq", "row"), pairs)


def line_body(own, one, two, three, mark, out):
    for k, part in enumerate((own, one, two, three)):
        out[k] = part[...]


def line_of(*parts):
    return pl.pallas_call(
        line_body,
        in_specs=[IN_VMEM] * 4 + [ANYWHERE],
        out_specs=IN_VMEM,
        out_shape=pltpu.HBM((4, ROWS, CH), BF16),
        compiler_params=SMALL,
        cost_estimate=pl.CostEstimate(flops=0, bytes_accessed=1 << 10, transcendentals=0),
    )(*parts)


def projected(entering, c, parts, blocks):
    hidden = hidden_of(entering, c, *parts)
    ua, db, held = far_parts(hidden, blocks)
    ua, db = shift(ua, "head", 1), shift(db, "head", -1)
    ub, da, keep, held = near_parts(hidden, held, blocks, NEXT)
    ub, da = shift(ub, "head", 1), shift(da, "head", -1)
    two, held = rest_parts(hidden, held, blocks, REST)
    sent = add(keep[0], after(ua, two))
    ua = shift(sent, "head", 1)
    sent = add(keep[1], after(db, sent))
    db = shift(sent, "head", -1)
    (one,) = rest_parts(after(hidden, sent), held, blocks, ())
    sent = add(two[0, 1], after(ub, one))
    ub = shift(sent, "head", 1)
    sent = add(two[1, 0], after(da, sent))
    da = shift(sent, "head", -1)
    sent = add(two[0, 0], after(ua, sent))
    ua = shift(sent, "head", 1)
    sent = add(two[1, 1], after(db, sent))
    db = shift(sent, "head", -1)
    sent = add(one[0, 1], after(ub, sent))
    ub = shift(sent, "head", 1)
    sent = add(one[1, 0], after(da, sent))
    da = shift(sent, "head", -1)
    sent = add(one[0, 0], after(ua, sent))
    ua = shift(sent, "head", 1)
    sent = add(one[1, 1], after(db, sent))
    db = shift(sent, "head", -1)
    up = jnp.concatenate([ua, ub]).astype(F32)
    down = jnp.concatenate([da, db]).astype(F32)
    return (one[2].reshape(2 * PIECE, TOK).astype(F32) + up + down).T.astype(BF16)


def shards(x, g, b, c, step, log_gate, skip, out_weight):
    near = [from_line(out_weight, 0, offset) for offset in (1, 2, 3)]
    payload = shard_state(x, b, step, log_gate)
    line = line_of(out_weight, *near, in_hbm(payload))
    one, three = (from_line(line, 1, offset) for offset in (1, 3))
    received = lax.all_to_all(payload.reshape(SHARDS, 8, HALF + P_SIZE), ("seq", "row"), 0, 0)
    parts = inner(x, g, b, c, step, log_gate, skip, payload)
    line, one, three = hold([line, one, three], received, in_hbm(parts[0]))
    two = from_line(line, 1, 2)
    other = [shift(v, "seq", 1) for v in (line, one, three)]
    half = lax.rem(lax.axis_index("row"), 2).reshape(1)
    slices = scan_shards(half, received, in_hbm(parts[0]))
    entering = lax.all_to_all(slices, ("seq", "row"), 0, 0)
    (two,) = hold([two], entering)
    other.insert(2, shift(two, "seq", 1))
    return projected(entering.reshape(16, 2, 8, HALF), c, parts, [line, one, two, three] + other)


def solution(mesh):
    return jax.shard_map(
        shards,
        mesh=mesh,
        in_specs=(
            P(("seq", "row"), "head"),
            P(("seq", "row"), "head"),
            P(("seq", "row"), None),
            P(("seq", "row"), None),
            P("head", ("seq", "row")),
            P("head", ("seq", "row")),
            P("head"),
            P(("seq", "row"), "head"),
        ),
        out_specs=P(("seq", "row"), "head"),
        check_vma=False,
    )
```

```python
import functools

import jax
import jax.numpy as jnp
from jax import lax
from jax.experimental import pallas as pl
from jax.experimental.pallas import tpu as pltpu
from jax.sharding import PartitionSpec as P

P_SIZE = 128
N = 128
BLK = 128
TOK = 768
HEADS = 10
CH = HEADS * P_SIZE
HALF = CH // 2
SHARDS = 32
ROWS = 80
PIECE = 160
FAR, NEAR, NEXT, REST = (4,), (3, -3), (2, -2), (1, -1, 0)
NBLK = TOK // BLK
F32 = jnp.float32
BF16 = jnp.bfloat16
HIGH = lax.Precision.HIGHEST
IN_VMEM = pl.BlockSpec(memory_space=pltpu.VMEM)
IN_SMEM = pl.BlockSpec(memory_space=pltpu.SMEM)
ANYWHERE = pl.BlockSpec(memory_space=pl.ANY)
SMALL = pltpu.CompilerParams(vmem_limit_bytes=24 << 20)
NT = (((1,), (1,)), ((), ()))
TN = (((0,), (0,)), ((), ()))


def in_vmem(value):
    return pltpu.with_memory_space_constraint(value, pltpu.VMEM)


def in_hbm(value):
    return pltpu.with_memory_space_constraint(value, pltpu.HBM)


def triangle(upto):
    rows = lax.broadcasted_iota(jnp.int32, (BLK, BLK), 0)
    cols = lax.broadcasted_iota(jnp.int32, (BLK, BLK), 1)
    return jnp.where(upto(rows, cols), 1.0, 0.0).astype(F32)


def columns_of():
    return lax.rem(lax.axis_index("row"), 4)


def rows_of():
    return lax.axis_index("row") // 4


def split3(value):
    high = value.astype(BF16)
    rest = value - high.astype(F32)
    mid = rest.astype(BF16)
    low = (rest - mid.astype(F32)).astype(BF16)
    return high, mid, low


def state_body(x_ref, b_ref, step_ref, log_ref, out_ref, tail_ref, decay_ref, turned_ref):
    half = pl.program_id(0)

    @pl.when(half == 0)
    def _():
        pad = jnp.zeros((16 - HEADS, BLK), F32)
        logs = log_ref[...]
        stacked = jnp.concatenate(
            [v for k in range(NBLK) for v in (logs[:, k * BLK : (k + 1) * BLK], pad)], axis=0
        )
        within = jnp.dot(stacked, triangle(lambda s, t: s > t), precision=HIGH, preferred_element_type=F32)
        sums = jnp.sum(stacked, axis=1, keepdims=True)
        suffix = jnp.zeros((16, 1), F32)
        pieces = [None] * NBLK
        for k in reversed(range(NBLK)):
            pieces[k] = within[16 * k : 16 * (k + 1)] + suffix
            suffix = suffix + sums[16 * k : 16 * (k + 1)]
        tail_ref[...] = jnp.exp(jnp.concatenate(pieces, axis=1)[:HEADS]) * step_ref[...]
        turned_ref[...] = jnp.transpose(b_ref[...].astype(F32))
        decay_ref[...] = jnp.broadcast_to(jnp.exp(suffix), (16, P_SIZE))

    turned = turned_ref[...]
    parts = []
    for j in range(HEADS // 2):
        row = tail_ref[pl.ds(half * (HEADS // 2) + j, 1), :]
        scaled = (turned * row).astype(BF16)
        here = slice(j * P_SIZE, (j + 1) * P_SIZE)
        parts.append(jnp.dot(scaled, x_ref[:, here], preferred_element_type=F32))
    state = jnp.concatenate(parts, axis=1).reshape(16, 8, HALF)
    rows = lax.broadcasted_iota(jnp.int32, (16, P_SIZE), 0)
    cols = lax.broadcasted_iota(jnp.int32, (16, P_SIZE), 1)
    line = jnp.sum(jnp.where(rows == cols, decay_ref[...], 0.0), axis=0, keepdims=True)
    high, mid, low = (v.astype(F32) for v in split3(line))
    which = lax.broadcasted_iota(jnp.int32, (8, P_SIZE), 0)
    extra = jnp.where(which == 0, high, jnp.where(which == 1, mid, jnp.where(which == 2, low, 0.0)))
    extra = jnp.broadcast_to(extra[None], (16, 8, P_SIZE))
    out_ref[:, 0] = jnp.concatenate([state, extra], axis=2).astype(BF16)


def shard_state(x, b, step, log_gate):
    return pl.pallas_call(
        state_body,
        grid=(2,),
        in_specs=[
            pl.BlockSpec((TOK, HALF), lambda i: (0, i)),
            pl.BlockSpec((TOK, N), lambda i: (0, 0)),
            pl.BlockSpec((HEADS, TOK), lambda i: (0, 0)),
            pl.BlockSpec((HEADS, TOK), lambda i: (0, 0)),
        ],
        out_specs=pl.BlockSpec((16, 1, 8, HALF + P_SIZE), lambda i: (0, i, 0, 0)),
        out_shape=pltpu.HBM((16, 2, 8, HALF + P_SIZE), BF16),
        scratch_shapes=[pltpu.VMEM((HEADS, TOK), F32), pltpu.VMEM((16, P_SIZE), F32), pltpu.VMEM((N, TOK), F32)],
        compiler_params=SMALL,
        cost_estimate=pl.CostEstimate(flops=2 * TOK * N * CH, bytes_accessed=3 << 20, transcendentals=0),
    )(*[in_hbm(v) for v in (x, b, step, log_gate)])


def scan_body(half_ref, in_ref, mark_ref, out_ref, decay_ref):
    lines = in_ref[:, :, HALF:].astype(F32)
    decay = jnp.sum(lines, axis=1)
    rows = lax.broadcasted_iota(jnp.int32, (P_SIZE, HALF), 0)
    cols = lax.broadcasted_iota(jnp.int32, (P_SIZE, HALF), 1)
    spread = jnp.where(rows == cols // P_SIZE + 5 * half_ref[0], 1.0, 0.0).astype(F32)
    decay_ref[...] = jnp.dot(decay, spread, precision=HIGH, preferred_element_type=F32)
    state = jnp.zeros((8, HALF), F32)
    for k in range(SHARDS):
        out_ref[k] = state.astype(BF16)
        state = decay_ref[k : k + 1, :] * state + in_ref[k, :, :HALF].astype(F32)


def scan_shards(half, received, mark):
    return pl.pallas_call(
        scan_body,
        in_specs=[
            IN_SMEM,
            IN_VMEM,
            ANYWHERE,
        ],
        out_specs=IN_VMEM,
        out_shape=pltpu.HBM((SHARDS, 8, HALF), BF16),
        scratch_shapes=[pltpu.VMEM((SHARDS, HALF), F32)],
        compiler_params=SMALL,
    )(half, received, mark)


def inner_body(x_ref, g_ref, b_ref, c_ref, step_ref, log_ref, skip_ref, mark_ref, pre_ref, gain_ref, state_ref, past_ref):
    k = pl.program_id(0)
    tokens = pl.ds(pl.multiple_of(k * BLK, BLK), BLK)

    @pl.when(k == 0)
    def _():
        state_ref[...] = jnp.zeros_like(state_ref)
        past_ref[...] = jnp.zeros_like(past_ref)

    logs = log_ref[...]
    steps = step_ref[...]
    upto = triangle(lambda s, t: s <= t)
    running = jnp.dot(logs, upto, precision=HIGH, preferred_element_type=F32)
    total = running[:, BLK - 1 :]
    tail = jnp.exp(total - running) * steps
    past = past_ref[...][:HEADS, :]
    pad = jnp.zeros((16 - HEADS, BLK), F32)
    columns = jnp.transpose(
        jnp.concatenate([running, pad, jnp.exp(running), pad, jnp.exp(running + past), pad], axis=0)
    )
    b_rows, c_rows = b_ref[...], c_ref[...]
    turned = jnp.transpose(b_rows.astype(F32))
    c_wide = c_rows.astype(F32)
    scores = lax.dot_general(c_rows, b_rows, NT, preferred_element_type=F32)
    rows = lax.broadcasted_iota(jnp.int32, (BLK, BLK), 0)
    cols = lax.broadcasted_iota(jnp.int32, (BLK, BLK), 1)
    causal = rows >= cols
    scores = jnp.where(causal, scores, 0.0)
    grow = jnp.exp(total)
    for h in range(HEADS):
        here = slice(h * P_SIZE, (h + 1) * P_SIZE)
        span = columns[:, h : h + 1] - running[h : h + 1, :]
        decays = jnp.exp(jnp.where(causal, span, 0.0))
        weight = (decays * scores * steps[h : h + 1, :]).astype(BF16)
        reach = (columns[:, 16 + h : 17 + h] * c_wide).astype(BF16)
        x_here = x_ref[:, here]
        state = state_ref[:, here]
        out = jnp.dot(
            jnp.concatenate([weight, reach], axis=1),
            jnp.concatenate([x_here, state.astype(BF16)], axis=0),
            preferred_element_type=F32,
        )
        out = out + skip_ref[0, h] * x_here.astype(F32)
        gate = g_ref[:, here].astype(F32)
        silu = 0.5 * gate * (1.0 + jnp.tanh(0.5 * gate))
        pre_ref[:, here] = (out * silu).astype(BF16)
        gain_ref[tokens, here] = (silu * columns[:, 32 + h : 33 + h]).astype(BF16)
        scaled = (turned * tail[h : h + 1, :]).astype(BF16)
        state_ref[:, here] = grow[h : h + 1, :] * state + jnp.dot(scaled, x_here, preferred_element_type=F32)
    past_ref[:HEADS, :] = past_ref[:HEADS, :] + total


def inner(x, g, b, c, step, log_gate, skip, mark):
    return pl.pallas_call(
        inner_body,
        grid=(NBLK,),
        in_specs=[
            pl.BlockSpec((BLK, CH), lambda i: (i, 0)),
            pl.BlockSpec((BLK, CH), lambda i: (i, 0)),
            pl.BlockSpec((BLK, N), lambda i: (i, 0)),
            pl.BlockSpec((BLK, N), lambda i: (i, 0)),
            pl.BlockSpec((HEADS, BLK), lambda i: (0, i)),
            pl.BlockSpec((HEADS, BLK), lambda i: (0, i)),
            IN_SMEM,
            ANYWHERE,
        ],
        out_specs=[pl.BlockSpec((BLK, CH), lambda i: (i, 0)), IN_VMEM],
        out_shape=[pltpu.HBM((TOK, CH), BF16), pltpu.VMEM((TOK, CH), BF16)],
        scratch_shapes=[pltpu.VMEM((N, CH), F32), pltpu.VMEM((16, BLK), F32)],
        compiler_params=SMALL,
        cost_estimate=pl.CostEstimate(flops=1 << 20, bytes_accessed=40 << 20, transcendentals=0),
    )(*[in_hbm(v) for v in (x, g, b, c, step, log_gate)], skip.reshape(1, HEADS), in_hbm(mark))


def hold_body(*refs):
    pass


def hold(values, *marks):
    count = len(values)
    return pl.pallas_call(
        hold_body,
        in_specs=[ANYWHERE] * (count + len(marks)),
        out_specs=[ANYWHERE] * count,
        out_shape=[pltpu.HBM(v.shape, v.dtype) for v in values],
        input_output_aliases={i: i for i in range(count)},
        compiler_params=SMALL,
        cost_estimate=pl.CostEstimate(flops=0, bytes_accessed=0, transcendentals=0),
    )(*[in_hbm(v) for v in values], *marks)


def fetch(refs, held, sems, ups):
    seq, head = lax.axis_index("seq"), lax.axis_index("head")
    for slot, up in enumerate(ups):
        group = lax.rem(head + (up + 8), 8)
        first = group < 4
        down = lax.rem(lax.rem(group, 4) - rows_of() + 4, 4)
        base = jnp.where((seq == 0) == first, 0, 4)
        for j in range(4):
            right = lax.rem(j - columns_of() + 4, 4)
            array = base + jnp.where(first, down, right)
            block = jnp.where(first, right, down)
            for k, ref in enumerate(refs):

                @pl.when(array == k)
                def _(ref=ref, block=block, slot=slot, j=j):
                    pltpu.make_async_copy(ref.at[block], held.at[slot, j], sems.at[slot, j]).start()


def arrive(refs, held, sems):
    for slot in range(held.shape[0]):
        for j in range(4):
            pltpu.make_async_copy(refs[0].at[0], held.at[slot, j], sems.at[slot, j]).wait()


def product(held, slot, hidden):
    rows = held[slot].reshape(4 * ROWS, CH)
    return lax.dot_general(rows, hidden, NT, preferred_element_type=F32).astype(BF16)


def held_weights(count):
    return pltpu.VMEM((count, 4, ROWS, CH), BF16)


def hidden_body(in_ref, c_ref, pre_ref, gain_ref, hidden_ref, state_ref):
    rows = c_ref.shape[0]
    here = pl.ds(pl.multiple_of(pl.program_id(0) * rows, rows), rows)

    @pl.when(pl.program_id(0) == 0)
    def _():
        for half in range(2):
            state_ref[half] = in_ref[:, half].astype(F32).reshape(N, HALF).astype(BF16)

    for half in range(2):
        cols = slice(half * HALF, (half + 1) * HALF)
        carried = jnp.dot(c_ref[...], state_ref[half], preferred_element_type=F32)
        hidden_ref[here, cols] = (pre_ref[:, cols].astype(F32) + gain_ref[here, cols].astype(F32) * carried).astype(BF16)


def hidden_of(entering, c, pre, gain):
    rows = 256
    return pl.pallas_call(
        hidden_body,
        grid=(TOK // rows,),
        in_specs=[
            pl.BlockSpec((16, 2, 8, HALF), lambda i: (0, 0, 0, 0)),
            pl.BlockSpec((rows, N), lambda i: (i, 0)),
            pl.BlockSpec((rows, CH), lambda i: (i, 0)),
            IN_VMEM,
        ],
        out_specs=IN_VMEM,
        out_shape=pltpu.VMEM((TOK, CH), BF16),
        scratch_shapes=[pltpu.VMEM((2, N, HALF), BF16)],
        compiler_params=SMALL,
        cost_estimate=pl.CostEstimate(flops=2 * TOK * N * CH, bytes_accessed=5 << 20, transcendentals=0),
    )(entering, *[in_hbm(v) for v in (c, pre)], in_vmem(gain))


def in_place(blocks):
    return [v if k == 6 else in_hbm(v) for k, v in enumerate(blocks)]


def far_body(hidden_ref, *refs):
    refs, (up_ref, down_ref, later, held, sems, later_sems) = refs[:8], refs[8:]
    fetch(refs, held, sems, FAR)
    fetch(refs, later, later_sems, NEAR)
    arrive(refs, held, sems)
    out = product(held, 0, hidden_ref[...])
    up_ref[...] = out[:PIECE]
    down_ref[...] = out[PIECE:]
    arrive(refs, later, later_sems)


def far_parts(hidden, blocks):
    return pl.pallas_call(
        far_body,
        in_specs=[IN_VMEM] + [ANYWHERE] * 8,
        out_specs=[IN_VMEM] * 3,
        out_shape=[jax.ShapeDtypeStruct((PIECE, TOK), BF16)] * 2 + [held_weights(2)],
        scratch_shapes=[held_weights(1), pltpu.SemaphoreType.DMA((1, 4)), pltpu.SemaphoreType.DMA((2, 4))],
        compiler_params=SMALL,
        cost_estimate=pl.CostEstimate(flops=2 * 320 * TOK * CH, bytes_accessed=2 << 20, transcendentals=0),
    )(in_vmem(hidden), *in_place(blocks))


def near_body(ups, hidden_ref, held, *refs):
    refs, (up_ref, down_ref, keep_ref, later, sems) = refs[:8], refs[8:]
    fetch(refs, later, sems, ups)
    out = product(held, 0, hidden_ref[...])
    up_ref[...] = out[PIECE:]
    keep_ref[0] = out[:PIECE]
    out = product(held, 1, hidden_ref[...])
    down_ref[...] = out[:PIECE]
    keep_ref[1] = out[PIECE:]
    arrive(refs, later, sems)


def near_parts(hidden, held, blocks, ups):
    return pl.pallas_call(
        functools.partial(near_body, ups),
        in_specs=[IN_VMEM, IN_VMEM] + [ANYWHERE] * 8,
        out_specs=[IN_VMEM] * 4,
        out_shape=[jax.ShapeDtypeStruct((PIECE, TOK), BF16)] * 2
        + [jax.ShapeDtypeStruct((2, PIECE, TOK), BF16), held_weights(len(ups))],
        scratch_shapes=[pltpu.SemaphoreType.DMA((len(ups), 4))],
        compiler_params=SMALL,
        cost_estimate=pl.CostEstimate(flops=4 * 320 * TOK * CH, bytes_accessed=2 << 20, transcendentals=0),
    )(in_vmem(hidden), in_vmem(held), *in_place(blocks))


def rest_body(ups, hidden_ref, held, *refs):
    refs, (out_ref, *scratch) = refs[:8], refs[8:]
    if ups:
        later, sems = scratch
        fetch(refs, later, sems, ups)
    for slot in range(held.shape[0]):
        out_ref[slot] = product(held, slot, hidden_ref[...]).reshape(2, PIECE, TOK)
    if ups:
        arrive(refs, later, sems)


def rest_parts(hidden, held, blocks, ups):
    count, later = held.shape[0], len(ups)
    return pl.pallas_call(
        functools.partial(rest_body, ups),
        in_specs=[IN_VMEM, IN_VMEM] + [ANYWHERE] * 8,
        out_specs=[IN_VMEM] * (2 if later else 1),
        out_shape=[jax.ShapeDtypeStruct((count, 2, PIECE, TOK), BF16)] + ([held_weights(later)] if later else []),
        scratch_shapes=[pltpu.SemaphoreType.DMA((later, 4))] if later else [],
        compiler_params=SMALL,
        cost_estimate=pl.CostEstimate(flops=2 * count * 320 * TOK * CH, bytes_accessed=count << 20, transcendentals=0),
    )(in_vmem(hidden), in_vmem(held), *in_place(blocks))


def shift(value, axis, by):
    size = lax.axis_size(axis)
    return lax.ppermute(value, axis, [(i, (i + by) % size) for i in range(size)])


def after(value, earlier):
    return lax.optimization_barrier((value, earlier))[0]


def add(a, b):
    return (a.astype(F32) + b.astype(F32)).astype(BF16)


def place(seq, y, x):
    return seq * 16 + y * 4 + x


def from_line(value, stage, offset):
    pairs = []
    for seq in range(2):
        for y in range(4):
            for x in range(4):
                if (seq == 0) == (stage == 0):
                    source = place(seq, y, (x + offset) % 4)
                else:
                    source = place(seq, (y + offset) % 4, x)
                pairs.append((source, place(seq, y, x)))
    return lax.ppermute(value, ("seq", "row"), pairs)


def line_body(own, one, two, three, mark, out):
    for k, part in enumerate((own, one, two, three)):
        out[k] = part[...]


def line_of(*parts):
    return pl.pallas_call(
        line_body,
        in_specs=[IN_VMEM] * 4 + [ANYWHERE],
        out_specs=IN_VMEM,
        out_shape=pltpu.HBM((4, ROWS, CH), BF16),
        compiler_params=SMALL,
        cost_estimate=pl.CostEstimate(flops=0, bytes_accessed=1 << 10, transcendentals=0),
    )(*parts)


def projected(entering, c, parts, blocks):
    hidden = hidden_of(entering, c, *parts)
    ua, db, held = far_parts(hidden, blocks)
    ua, db = shift(ua, "head", 1), shift(db, "head", -1)
    ub, da, keep, held = near_parts(hidden, held, blocks, NEXT)
    ub, da = shift(ub, "head", 1), shift(da, "head", -1)
    two, held = rest_parts(hidden, held, blocks, REST)
    sent = add(keep[0], after(ua, two))
    ua = shift(sent, "head", 1)
    sent = add(keep[1], after(db, sent))
    db = shift(sent, "head", -1)
    (one,) = rest_parts(after(hidden, sent), held, blocks, ())
    sent = add(two[0, 1], after(ub, one))
    ub = shift(sent, "head", 1)
    sent = add(two[1, 0], after(da, sent))
    da = shift(sent, "head", -1)
    sent = add(two[0, 0], after(ua, sent))
    ua = shift(sent, "head", 1)
    sent = add(two[1, 1], after(db, sent))
    db = shift(sent, "head", -1)
    sent = add(one[0, 1], after(ub, sent))
    ub = shift(sent, "head", 1)
    sent = add(one[1, 0], after(da, sent))
    da = shift(sent, "head", -1)
    sent = add(one[0, 0], after(ua, sent))
    ua = shift(sent, "head", 1)
    sent = add(one[1, 1], after(db, sent))
    db = shift(sent, "head", -1)
    up = jnp.concatenate([ua, ub]).astype(F32)
    down = jnp.concatenate([da, db]).astype(F32)
    return (one[2].reshape(2 * PIECE, TOK).astype(F32) + up + down).T.astype(BF16)


def shards(x, g, b, c, step, log_gate, skip, out_weight):
    near = [from_line(out_weight, 0, offset) for offset in (1, 2, 3)]
    payload = shard_state(x, b, step, log_gate)
    line = line_of(out_weight, *near, in_hbm(payload))
    one, three = (from_line(line, 1, offset) for offset in (1, 3))
    received = lax.all_to_all(payload.reshape(SHARDS, 8, HALF + P_SIZE), ("seq", "row"), 0, 0)
    parts = inner(x, g, b, c, step, log_gate, skip, payload)
    line, one, three = hold([line, one, three], received, in_hbm(parts[0]))
    two = from_line(line, 1, 2)
    other = [shift(v, "seq", 1) for v in (line, one, three)]
    half = lax.rem(lax.axis_index("row"), 2).reshape(1)
    slices = scan_shards(half, received, in_hbm(parts[0]))
    entering = lax.all_to_all(slices, ("seq", "row"), 0, 0)
    (two,) = hold([two], entering)
    other.insert(2, shift(two, "seq", 1))
    return projected(entering.reshape(16, 2, 8, HALF), c, parts, [line, one, two, three] + other)


def solution(mesh):
    return jax.shard_map(
        shards,
        mesh=mesh,
        in_specs=(
            P(("seq", "row"), "head"),
            P(("seq", "row"), "head"),
            P(("seq", "row"), None),
            P(("seq", "row"), None),
            P("head", ("seq", "row")),
            P("head", ("seq", "row")),
            P("head"),
            P(("seq", "row"), "head"),
        ),
        out_specs=P(("seq", "row"), "head"),
        check_vma=False,
    )
```

```python
import functools

import jax
import jax.numpy as jnp
from jax import lax
from jax.experimental import pallas as pl
from jax.experimental.pallas import tpu as pltpu
from jax.sharding import PartitionSpec as P

P_SIZE = 128
N = 128
BLK = 128
TOK = 768
HEADS = 10
CH = HEADS * P_SIZE
HALF = CH // 2
SHARDS = 32
ROWS = 80
PIECE = 160
KEPT = 2
FAR, NEAR, NEXT, REST = (4,), (3, -3), (2, -2), (1, -1, 0)
NBLK = TOK // BLK
F32 = jnp.float32
BF16 = jnp.bfloat16
HIGH = lax.Precision.HIGHEST
IN_VMEM = pl.BlockSpec(memory_space=pltpu.VMEM)
IN_SMEM = pl.BlockSpec(memory_space=pltpu.SMEM)
ANYWHERE = pl.BlockSpec(memory_space=pl.ANY)
SMALL = pltpu.CompilerParams(vmem_limit_bytes=24 << 20)
NT = (((1,), (1,)), ((), ()))
TN = (((0,), (0,)), ((), ()))


def in_vmem(value):
    return pltpu.with_memory_space_constraint(value, pltpu.VMEM)


def in_hbm(value):
    return pltpu.with_memory_space_constraint(value, pltpu.HBM)


def triangle(upto):
    rows = lax.broadcasted_iota(jnp.int32, (BLK, BLK), 0)
    cols = lax.broadcasted_iota(jnp.int32, (BLK, BLK), 1)
    return jnp.where(upto(rows, cols), 1.0, 0.0).astype(F32)


def columns_of():
    return lax.rem(lax.axis_index("row"), 4)


def rows_of():
    return lax.axis_index("row") // 4


def split3(value):
    high = value.astype(BF16)
    rest = value - high.astype(F32)
    mid = rest.astype(BF16)
    low = (rest - mid.astype(F32)).astype(BF16)
    return high, mid, low


def state_body(x_ref, b_ref, step_ref, log_ref, out_ref, tail_ref, decay_ref, turned_ref):
    half = pl.program_id(0)

    @pl.when(half == 0)
    def _():
        pad = jnp.zeros((16 - HEADS, BLK), F32)
        logs = log_ref[...]
        stacked = jnp.concatenate(
            [v for k in range(NBLK) for v in (logs[:, k * BLK : (k + 1) * BLK], pad)], axis=0
        )
        within = jnp.dot(stacked, triangle(lambda s, t: s > t), precision=HIGH, preferred_element_type=F32)
        sums = jnp.sum(stacked, axis=1, keepdims=True)
        suffix = jnp.zeros((16, 1), F32)
        pieces = [None] * NBLK
        for k in reversed(range(NBLK)):
            pieces[k] = within[16 * k : 16 * (k + 1)] + suffix
            suffix = suffix + sums[16 * k : 16 * (k + 1)]
        tail_ref[...] = jnp.exp(jnp.concatenate(pieces, axis=1)[:HEADS]) * step_ref[...]
        turned_ref[...] = jnp.transpose(b_ref[...].astype(F32))
        decay_ref[...] = jnp.broadcast_to(jnp.exp(suffix), (16, P_SIZE))

    turned = turned_ref[...]
    parts = []
    for j in range(HEADS // 2):
        row = tail_ref[pl.ds(half * (HEADS // 2) + j, 1), :]
        scaled = (turned * row).astype(BF16)
        here = slice(j * P_SIZE, (j + 1) * P_SIZE)
        parts.append(jnp.dot(scaled, x_ref[:, here], preferred_element_type=F32))
    state = jnp.concatenate(parts, axis=1).reshape(16, 8, HALF)
    rows = lax.broadcasted_iota(jnp.int32, (16, P_SIZE), 0)
    cols = lax.broadcasted_iota(jnp.int32, (16, P_SIZE), 1)
    line = jnp.sum(jnp.where(rows == cols, decay_ref[...], 0.0), axis=0, keepdims=True)
    high, mid, low = (v.astype(F32) for v in split3(line))
    which = lax.broadcasted_iota(jnp.int32, (8, P_SIZE), 0)
    extra = jnp.where(which == 0, high, jnp.where(which == 1, mid, jnp.where(which == 2, low, 0.0)))
    extra = jnp.broadcast_to(extra[None], (16, 8, P_SIZE))
    out_ref[:, 0] = jnp.concatenate([state, extra], axis=2).astype(BF16)


def shard_state(x, b, step, log_gate):
    return pl.pallas_call(
        state_body,
        grid=(2,),
        in_specs=[
            pl.BlockSpec((TOK, HALF), lambda i: (0, i)),
            pl.BlockSpec((TOK, N), lambda i: (0, 0)),
            pl.BlockSpec((HEADS, TOK), lambda i: (0, 0)),
            pl.BlockSpec((HEADS, TOK), lambda i: (0, 0)),
        ],
        out_specs=pl.BlockSpec((16, 1, 8, HALF + P_SIZE), lambda i: (0, i, 0, 0)),
        out_shape=pltpu.HBM((16, 2, 8, HALF + P_SIZE), BF16),
        scratch_shapes=[pltpu.VMEM((HEADS, TOK), F32), pltpu.VMEM((16, P_SIZE), F32), pltpu.VMEM((N, TOK), F32)],
        compiler_params=SMALL,
        cost_estimate=pl.CostEstimate(flops=2 * TOK * N * CH, bytes_accessed=3 << 20, transcendentals=0),
    )(*[in_hbm(v) for v in (x, b, step, log_gate)])


def scan_body(half_ref, in_ref, mark_ref, out_ref, decay_ref):
    lines = in_ref[:, :, HALF:].astype(F32)
    decay = jnp.sum(lines, axis=1)
    rows = lax.broadcasted_iota(jnp.int32, (P_SIZE, HALF), 0)
    cols = lax.broadcasted_iota(jnp.int32, (P_SIZE, HALF), 1)
    spread = jnp.where(rows == cols // P_SIZE + 5 * half_ref[0], 1.0, 0.0).astype(F32)
    decay_ref[...] = jnp.dot(decay, spread, precision=HIGH, preferred_element_type=F32)
    state = jnp.zeros((8, HALF), F32)
    for k in range(SHARDS):
        out_ref[k] = state.astype(BF16)
        state = decay_ref[k : k + 1, :] * state + in_ref[k, :, :HALF].astype(F32)


def scan_shards(half, received, mark):
    return pl.pallas_call(
        scan_body,
        in_specs=[
            IN_SMEM,
            IN_VMEM,
            ANYWHERE,
        ],
        out_specs=IN_VMEM,
        out_shape=pltpu.HBM((SHARDS, 8, HALF), BF16),
        scratch_shapes=[pltpu.VMEM((SHARDS, HALF), F32)],
        compiler_params=SMALL,
    )(half, received, mark)


def inner_body(x_ref, g_ref, b_ref, c_ref, step_ref, log_ref, skip_ref, mark_ref, near_ref, pre_ref, gain_ref, state_ref, past_ref):
    k = pl.program_id(0)
    tokens = pl.ds(pl.multiple_of(k * BLK, BLK), BLK)
    kept = pl.ds(pl.multiple_of(jnp.minimum(k, KEPT) * BLK, BLK), BLK)

    @pl.when(k == 0)
    def _():
        state_ref[...] = jnp.zeros_like(state_ref)
        past_ref[...] = jnp.zeros_like(past_ref)

    logs = log_ref[...]
    steps = step_ref[...]
    upto = triangle(lambda s, t: s <= t)
    running = jnp.dot(logs, upto, precision=HIGH, preferred_element_type=F32)
    total = running[:, BLK - 1 :]
    tail = jnp.exp(total - running) * steps
    past = past_ref[...][:HEADS, :]
    pad = jnp.zeros((16 - HEADS, BLK), F32)
    columns = jnp.transpose(
        jnp.concatenate([running, pad, jnp.exp(running), pad, jnp.exp(running + past), pad], axis=0)
    )
    b_rows, c_rows = b_ref[...], c_ref[...]
    turned = jnp.transpose(b_rows.astype(F32))
    c_wide = c_rows.astype(F32)
    scores = lax.dot_general(c_rows, b_rows, NT, preferred_element_type=F32)
    rows = lax.broadcasted_iota(jnp.int32, (BLK, BLK), 0)
    cols = lax.broadcasted_iota(jnp.int32, (BLK, BLK), 1)
    causal = rows >= cols
    scores = jnp.where(causal, scores, 0.0)
    grow = jnp.exp(total)
    for h in range(HEADS):
        here = slice(h * P_SIZE, (h + 1) * P_SIZE)
        span = columns[:, h : h + 1] - running[h : h + 1, :]
        decays = jnp.exp(jnp.where(causal, span, 0.0))
        weight = (decays * scores * steps[h : h + 1, :]).astype(BF16)
        reach = (columns[:, 16 + h : 17 + h] * c_wide).astype(BF16)
        x_here = x_ref[:, here]
        state = state_ref[:, here]
        out = jnp.dot(
            jnp.concatenate([weight, reach], axis=1),
            jnp.concatenate([x_here, state.astype(BF16)], axis=0),
            preferred_element_type=F32,
        )
        out = out + skip_ref[0, h] * x_here.astype(F32)
        gate = g_ref[:, here].astype(F32)
        silu = 0.5 * gate * (1.0 + jnp.tanh(0.5 * gate))
        pre = (out * silu).astype(BF16)
        near_ref[kept, here] = pre
        pre_ref[:, here] = pre
        gain_ref[tokens, here] = (silu * columns[:, 32 + h : 33 + h]).astype(BF16)
        scaled = (turned * tail[h : h + 1, :]).astype(BF16)
        state_ref[:, here] = grow[h : h + 1, :] * state + jnp.dot(scaled, x_here, preferred_element_type=F32)
    past_ref[:HEADS, :] = past_ref[:HEADS, :] + total


def inner(x, g, b, c, step, log_gate, skip, mark):
    return pl.pallas_call(
        inner_body,
        grid=(NBLK,),
        in_specs=[
            pl.BlockSpec((BLK, CH), lambda i: (i, 0)),
            pl.BlockSpec((BLK, CH), lambda i: (i, 0)),
            pl.BlockSpec((BLK, N), lambda i: (i, 0)),
            pl.BlockSpec((BLK, N), lambda i: (i, 0)),
            pl.BlockSpec((HEADS, BLK), lambda i: (0, i)),
            pl.BlockSpec((HEADS, BLK), lambda i: (0, i)),
            IN_SMEM,
            ANYWHERE,
        ],
        out_specs=[IN_VMEM, pl.BlockSpec((BLK, CH), lambda i: (jnp.maximum(i - KEPT, 0), 0)), IN_VMEM],
        out_shape=[
            pltpu.VMEM(((KEPT + 1) * BLK, CH), BF16),
            pltpu.HBM((TOK - KEPT * BLK, CH), BF16),
            pltpu.VMEM((TOK, CH), BF16),
        ],
        scratch_shapes=[pltpu.VMEM((N, CH), F32), pltpu.VMEM((16, BLK), F32)],
        compiler_params=SMALL,
        cost_estimate=pl.CostEstimate(flops=1 << 20, bytes_accessed=40 << 20, transcendentals=0),
    )(*[in_hbm(v) for v in (x, g, b, c, step, log_gate)], skip.reshape(1, HEADS), in_hbm(mark))


def hold_body(*refs):
    pass


def hold(values, *marks):
    count = len(values)
    return pl.pallas_call(
        hold_body,
        in_specs=[ANYWHERE] * (count + len(marks)),
        out_specs=[ANYWHERE] * count,
        out_shape=[pltpu.HBM(v.shape, v.dtype) for v in values],
        input_output_aliases={i: i for i in range(count)},
        compiler_params=SMALL,
        cost_estimate=pl.CostEstimate(flops=0, bytes_accessed=0, transcendentals=0),
    )(*[in_hbm(v) for v in values], *marks)


def fetch(refs, held, sems, ups):
    seq, head = lax.axis_index("seq"), lax.axis_index("head")
    for slot, up in enumerate(ups):
        group = lax.rem(head + (up + 8), 8)
        first = group < 4
        down = lax.rem(lax.rem(group, 4) - rows_of() + 4, 4)
        base = jnp.where((seq == 0) == first, 0, 4)
        for j in range(4):
            right = lax.rem(j - columns_of() + 4, 4)
            array = base + jnp.where(first, down, right)
            block = jnp.where(first, right, down)
            for k, ref in enumerate(refs):

                @pl.when(array == k)
                def _(ref=ref, block=block, slot=slot, j=j):
                    pltpu.make_async_copy(ref.at[block], held.at[slot, j], sems.at[slot, j]).start()


def arrive(refs, held, sems):
    for slot in range(held.shape[0]):
        for j in range(4):
            pltpu.make_async_copy(refs[0].at[0], held.at[slot, j], sems.at[slot, j]).wait()


def product(held, slot, hidden):
    rows = held[slot].reshape(4 * ROWS, CH)
    return lax.dot_general(rows, hidden, NT, preferred_element_type=F32).astype(BF16)


def held_weights(count):
    return pltpu.VMEM((count, 4, ROWS, CH), BF16)


def hidden_body(in_ref, c_ref, near_ref, pre_ref, gain_ref, hidden_ref, state_ref):
    rows = c_ref.shape[0]
    here = pl.ds(pl.multiple_of(pl.program_id(0) * rows, rows), rows)

    @pl.when(pl.program_id(0) == 0)
    def _():
        for half in range(2):
            state_ref[half] = in_ref[:, half].astype(F32).reshape(N, HALF).astype(BF16)

    for half in range(2):
        cols = slice(half * HALF, (half + 1) * HALF)
        carried = jnp.dot(c_ref[...], state_ref[half], preferred_element_type=F32)
        pre = jnp.where(pl.program_id(0) == 0, near_ref[:rows, cols], pre_ref[:, cols])
        hidden_ref[here, cols] = (pre.astype(F32) + gain_ref[here, cols].astype(F32) * carried).astype(BF16)


def hidden_of(entering, c, near, pre, gain):
    rows = KEPT * BLK
    return pl.pallas_call(
        hidden_body,
        grid=(TOK // rows,),
        in_specs=[
            pl.BlockSpec((16, 2, 8, HALF), lambda i: (0, 0, 0, 0)),
            pl.BlockSpec((rows, N), lambda i: (i, 0)),
            IN_VMEM,
            pl.BlockSpec((rows, CH), lambda i: (jnp.maximum(i - 1, 0), 0)),
            IN_VMEM,
        ],
        out_specs=IN_VMEM,
        out_shape=pltpu.VMEM((TOK, CH), BF16),
        scratch_shapes=[pltpu.VMEM((2, N, HALF), BF16)],
        compiler_params=SMALL,
        cost_estimate=pl.CostEstimate(flops=2 * TOK * N * CH, bytes_accessed=5 << 20, transcendentals=0),
    )(entering, in_hbm(c), in_vmem(near), in_hbm(pre), in_vmem(gain))


def in_place(blocks):
    return [v if k == 6 else in_hbm(v) for k, v in enumerate(blocks)]


def far_body(hidden_ref, *refs):
    refs, (up_ref, down_ref, later, held, sems, later_sems) = refs[:8], refs[8:]
    fetch(refs, held, sems, FAR)
    fetch(refs, later, later_sems, NEAR)
    arrive(refs, held, sems)
    out = product(held, 0, hidden_ref[...])
    up_ref[...] = out[:PIECE]
    down_ref[...] = out[PIECE:]
    arrive(refs, later, later_sems)


def far_parts(hidden, blocks):
    return pl.pallas_call(
        far_body,
        in_specs=[IN_VMEM] + [ANYWHERE] * 8,
        out_specs=[IN_VMEM] * 3,
        out_shape=[jax.ShapeDtypeStruct((PIECE, TOK), BF16)] * 2 + [held_weights(2)],
        scratch_shapes=[held_weights(1), pltpu.SemaphoreType.DMA((1, 4)), pltpu.SemaphoreType.DMA((2, 4))],
        compiler_params=SMALL,
        cost_estimate=pl.CostEstimate(flops=2 * 320 * TOK * CH, bytes_accessed=2 << 20, transcendentals=0),
    )(in_vmem(hidden), *in_place(blocks))


def near_body(ups, hidden_ref, held, *refs):
    refs, (up_ref, down_ref, keep_ref, later, sems) = refs[:8], refs[8:]
    fetch(refs, later, sems, ups)
    out = product(held, 0, hidden_ref[...])
    up_ref[...] = out[PIECE:]
    keep_ref[0] = out[:PIECE]
    out = product(held, 1, hidden_ref[...])
    down_ref[...] = out[:PIECE]
    keep_ref[1] = out[PIECE:]
    arrive(refs, later, sems)


def near_parts(hidden, held, blocks, ups):
    return pl.pallas_call(
        functools.partial(near_body, ups),
        in_specs=[IN_VMEM, IN_VMEM] + [ANYWHERE] * 8,
        out_specs=[IN_VMEM] * 4,
        out_shape=[jax.ShapeDtypeStruct((PIECE, TOK), BF16)] * 2
        + [jax.ShapeDtypeStruct((2, PIECE, TOK), BF16), held_weights(len(ups))],
        scratch_shapes=[pltpu.SemaphoreType.DMA((len(ups), 4))],
        compiler_params=SMALL,
        cost_estimate=pl.CostEstimate(flops=4 * 320 * TOK * CH, bytes_accessed=2 << 20, transcendentals=0),
    )(in_vmem(hidden), in_vmem(held), *in_place(blocks))


def rest_body(ups, hidden_ref, held, *refs):
    refs, (out_ref, *scratch) = refs[:8], refs[8:]
    if ups:
        later, sems = scratch
        fetch(refs, later, sems, ups)
    for slot in range(held.shape[0]):
        out_ref[slot] = product(held, slot, hidden_ref[...]).reshape(2, PIECE, TOK)
    if ups:
        arrive(refs, later, sems)


def rest_parts(hidden, held, blocks, ups):
    count, later = held.shape[0], len(ups)
    return pl.pallas_call(
        functools.partial(rest_body, ups),
        in_specs=[IN_VMEM, IN_VMEM] + [ANYWHERE] * 8,
        out_specs=[IN_VMEM] * (2 if later else 1),
        out_shape=[jax.ShapeDtypeStruct((count, 2, PIECE, TOK), BF16)] + ([held_weights(later)] if later else []),
        scratch_shapes=[pltpu.SemaphoreType.DMA((later, 4))] if later else [],
        compiler_params=SMALL,
        cost_estimate=pl.CostEstimate(flops=2 * count * 320 * TOK * CH, bytes_accessed=count << 20, transcendentals=0),
    )(in_vmem(hidden), in_vmem(held), *in_place(blocks))


def shift(value, axis, by):
    size = lax.axis_size(axis)
    return lax.ppermute(value, axis, [(i, (i + by) % size) for i in range(size)])


def after(value, earlier):
    return lax.optimization_barrier((value, earlier))[0]


def add(a, b):
    return (a.astype(F32) + b.astype(F32)).astype(BF16)


def place(seq, y, x):
    return seq * 16 + y * 4 + x


def from_line(value, stage, offset):
    pairs = []
    for seq in range(2):
        for y in range(4):
            for x in range(4):
                if (seq == 0) == (stage == 0):
                    source = place(seq, y, (x + offset) % 4)
                else:
                    source = place(seq, (y + offset) % 4, x)
                pairs.append((source, place(seq, y, x)))
    return lax.ppermute(value, ("seq", "row"), pairs)


def line_body(own, one, two, three, mark, out):
    for k, part in enumerate((own, one, two, three)):
        out[k] = part[...]


def line_of(*parts):
    return pl.pallas_call(
        line_body,
        in_specs=[IN_VMEM] * 4 + [ANYWHERE],
        out_specs=IN_VMEM,
        out_shape=pltpu.HBM((4, ROWS, CH), BF16),
        compiler_params=SMALL,
        cost_estimate=pl.CostEstimate(flops=0, bytes_accessed=1 << 10, transcendentals=0),
    )(*parts)


def projected(entering, c, parts, blocks):
    hidden = hidden_of(entering, c, *parts)
    ua, db, held = far_parts(hidden, blocks)
    ua, db = shift(ua, "head", 1), shift(db, "head", -1)
    ub, da, keep, held = near_parts(hidden, held, blocks, NEXT)
    ub, da = shift(ub, "head", 1), shift(da, "head", -1)
    two, held = rest_parts(hidden, held, blocks, REST)
    sent = add(keep[0], after(ua, two))
    ua = shift(sent, "head", 1)
    sent = add(keep[1], after(db, sent))
    db = shift(sent, "head", -1)
    (one,) = rest_parts(after(hidden, sent), held, blocks, ())
    sent = add(two[0, 1], after(ub, one))
    ub = shift(sent, "head", 1)
    sent = add(two[1, 0], after(da, sent))
    da = shift(sent, "head", -1)
    sent = add(two[0, 0], after(ua, sent))
    ua = shift(sent, "head", 1)
    sent = add(two[1, 1], after(db, sent))
    db = shift(sent, "head", -1)
    sent = add(one[0, 1], after(ub, sent))
    ub = shift(sent, "head", 1)
    sent = add(one[1, 0], after(da, sent))
    da = shift(sent, "head", -1)
    sent = add(one[0, 0], after(ua, sent))
    ua = shift(sent, "head", 1)
    sent = add(one[1, 1], after(db, sent))
    db = shift(sent, "head", -1)
    up = jnp.concatenate([ua, ub]).astype(F32)
    down = jnp.concatenate([da, db]).astype(F32)
    return (one[2].reshape(2 * PIECE, TOK).astype(F32) + up + down).T.astype(BF16)


def shards(x, g, b, c, step, log_gate, skip, out_weight):
    near = [from_line(out_weight, 0, offset) for offset in (1, 2, 3)]
    payload = shard_state(x, b, step, log_gate)
    line = line_of(out_weight, *near, in_hbm(payload))
    one, three = (from_line(line, 1, offset) for offset in (1, 3))
    received = lax.all_to_all(payload.reshape(SHARDS, 8, HALF + P_SIZE), ("seq", "row"), 0, 0)
    parts = inner(x, g, b, c, step, log_gate, skip, payload)
    line, one, three = hold([line, one, three], received, in_hbm(parts[1]))
    two = from_line(line, 1, 2)
    other = [shift(v, "seq", 1) for v in (line, one, three)]
    half = lax.rem(lax.axis_index("row"), 2).reshape(1)
    slices = scan_shards(half, received, in_hbm(parts[1]))
    entering = lax.all_to_all(slices, ("seq", "row"), 0, 0)
    (two,) = hold([two], entering)
    other.insert(2, shift(two, "seq", 1))
    return projected(entering.reshape(16, 2, 8, HALF), c, parts, [line, one, two, three] + other)


def solution(mesh):
    return jax.shard_map(
        shards,
        mesh=mesh,
        in_specs=(
            P(("seq", "row"), "head"),
            P(("seq", "row"), "head"),
            P(("seq", "row"), None),
            P(("seq", "row"), None),
            P("head", ("seq", "row")),
            P("head", ("seq", "row")),
            P("head"),
            P(("seq", "row"), "head"),
        ),
        out_specs=P(("seq", "row"), "head"),
        check_vma=False,
    )
```
